32 devices in a mesh: seq: 8 (over z, x), head: 4 (over y, core).
Axes of the slice: x: 2, y: 2, z: 4, core: 2. Of those that a mesh axis runs over, the one named last changes fastest.
Arguments:
- tokens: bfloat16 [2, 1024, 1024], P(None, 'seq', 'head'), may hold values from -6 to 6
- input_norm_gain: float32 [1024], replicated, may hold values from 0.1 to 1.9
- query_key_value_weight: bfloat16 [1024, 3, 1024], P(None, None, 'head'), may hold values from -0.1875 to 0.1875
- forget_gate_weight: bfloat16 [1024, 1024], P(None, 'head'), may hold values from -0.1875 to 0.1875
- convolution_filter_taps: float32 [2, 4, 3, 1024], P(None, None, None, 'head'), may hold values from -3 to 3
- slot_forget_rate: float32 [16, 64], P('head'), may hold values from 1.953125e-05 to 0.04
- extra_forget_log: float32 [2, 1024], P(None, 'seq'), may hold values from 0 to 1.4, as said below
- head_norm_gain: float32 [16, 64], P('head'), may hold values from 0.1 to 1.9
- output_projection_weight: bfloat16 [1024, 1024], P('head'), may hold values from -0.1875 to 0.1875
- feedforward_norm_gain: float32 [1024], replicated, may hold values from 0.1 to 1.9
- up_projection_weight: bfloat16 [1024, 4096], P(None, 'head'), may hold values from -0.1875 to 0.1875
- down_projection_weight: bfloat16 [4096, 1024], P('head'), may hold values from -0.09375 to 0.09375
Outputs:
- layer_out: bfloat16 [2, 1024, 1024], P(None, 'seq', 'head')
The draws below stay inside these ranges and needn't reach their ends.
Inputs may be any that keep to these rules, and one draw needn't show every extreme that they name: `extra_forget_log`: one value per position of a sequence, zero at most positions.
All inputs are finite; a program needn't handle non-finite values.
Results may differ from the reference program's by a relative error of at most 0.01.
Values may be sent and summed in bfloat16 or wider, within the bound.
A program may use at most 128 MiB of HBM per device.

```python
import jax
import jax.numpy as jnp
from jax import lax

D = 1024
HEADS = 16
HD = 64
SLOTS = 64
FF = 4096
SPAN = 64
BATCH = 2
SEQ_LEN = 1024


def draw_slot_forget_rate(key, part):
    first, second, third = jax.random.split(jax.random.fold_in(key, 11), 3)
    choose = jax.random.uniform(first, (HEADS, SLOTS), dtype=jnp.float32)
    share = 0.5
    slower = jnp.exp(jax.random.uniform(second, (HEADS, SLOTS), jnp.float32, jnp.log(0.02), jnp.log(0.4))) / SEQ_LEN
    faster = jnp.exp(jax.random.uniform(third, (HEADS, SLOTS), jnp.float32, jnp.log(0.02), jnp.log(0.04)))
    return jnp.where(choose < share, slower, faster).astype(jnp.float32)


def draw_extra_forget_log(key, part):
    first, second = jax.random.split(jax.random.fold_in(key, 23))
    places = jax.random.randint(first, (BATCH, 2), 0, SEQ_LEN)
    depth = jax.random.uniform(second, (BATCH, 2), jnp.float32, 0.22, 0.7)
    hitting = jnp.arange(SEQ_LEN)[None, None, :] == places[:, :, None]
    return jnp.sum(jnp.where(hitting, depth[:, :, None], 0.0), axis=1).astype(jnp.float32)


def steps_of(key, dims, cuts, least, largest):
    level, own = 1.0, jax.random.fold_in(key, 6)
    for position, shards_of in cuts:
        heights = jnp.exp(jax.random.uniform(jax.random.fold_in(own, position), (shards_of,), jnp.float32, least / len(cuts), largest / len(cuts)))
        level = level * jnp.repeat(heights, dims[position] // shards_of).reshape([-1 if axis == position else 1 for axis in range(len(dims))])
    return level


def gaussian(stream_key, extent, scale, bound, shards=(), kind=jnp.bfloat16):
    values = scale * jax.random.normal(stream_key, extent, jnp.float32)
    if shards:
        values = values * steps_of(stream_key, extent, shards, -0.22, 0.18)
    return jnp.clip(values, -bound, bound).astype(kind)


def setup_inputs(seed: int = 0) -> dict:
    keys = jax.random.split(jax.random.key(seed), 13)
    return {
        "tokens": gaussian(keys[0], (BATCH, SEQ_LEN, D), 1.0, 6.0, ((1, 8), (2, 4))),
        "input_norm_gain": jnp.clip(1.0 + 0.18 * jax.random.normal(keys[1], (D,), jnp.float32), 0.1, 1.9),
        "query_key_value_weight": gaussian(keys[2], (D, 3, HEADS * HD), D ** -0.5, 0.1875, ((2, 4),)),
        "forget_gate_weight": gaussian(keys[3], (D, HEADS * SLOTS), D ** -0.5, 0.1875, ((1, 4),)),
        "convolution_filter_taps": gaussian(keys[4], (2, 4, 3, HEADS * HD), 0.6, 3.0, ((3, 4),), jnp.float32),
        "slot_forget_rate": draw_slot_forget_rate(jax.random.fold_in(keys[12], 71), 0),
        "extra_forget_log": draw_extra_forget_log(jax.random.fold_in(keys[12], 71), 0),
        "head_norm_gain": jnp.clip(1.0 + 0.18 * jax.random.normal(keys[7], (HEADS, HD), jnp.float32), 0.1, 1.9),
        "output_projection_weight": gaussian(keys[8], (HEADS * HD, D), (HEADS * HD) ** -0.5, 0.1875, ((0, 4),)),
        "feedforward_norm_gain": jnp.clip(1.0 + 0.18 * jax.random.normal(keys[9], (D,), jnp.float32), 0.1, 1.9),
        "up_projection_weight": gaussian(keys[10], (D, FF), D ** -0.5, 0.1875, ((1, 4),)),
        "down_projection_weight": gaussian(keys[11], (FF, D), FF ** -0.5, 0.09375, ((0, 4),)),
    }


EPSILON = 1e-06
HIGHEST = lax.Precision.HIGHEST

def normalize(values, gain):
    return values * lax.rsqrt(lax.optimization_barrier(jnp.mean(values * values, axis=-1, keepdims=True)) + EPSILON) * gain

def convolve(padded, taps, backward):
    length = padded.shape[1] - 6
    running = jnp.zeros((padded.shape[0], length, padded.shape[2]), jnp.float32)
    for offset in range(4):
        first_row = 3 + offset if backward else 3 - offset
        running = running + taps[offset] * padded[:, first_row:first_row + length]
    return jax.nn.silu(running).astype(jnp.bfloat16)

def split_heads(mixed, head_count, head_size):
    grouped = mixed.astype(jnp.float32).reshape(mixed.shape[0], mixed.shape[1], 3, head_count, head_size)
    grouped = jnp.transpose(grouped, (2, 0, 3, 1, 4))
    return (grouped[0], grouped[1], grouped[2])

def log_decay_values(gate_scores, slot_forget_rate, extra_forget_log):
    head_count, slot_count = slot_forget_rate.shape
    gate_opening = jax.nn.sigmoid(gate_scores.reshape(gate_scores.shape[0], gate_scores.shape[1], head_count, slot_count))
    log_decay_total = -2.0 * slot_forget_rate * gate_opening - extra_forget_log[:, :, None, None]
    return jnp.transpose(log_decay_total, (0, 2, 1, 3))

def flipped(array):
    return jnp.flip(array, axis=2)

def span_pass(state, block):
    queries, keys_in, values, log_decay_total = block
    state_key, state_value = state
    cumulative = jnp.cumsum(log_decay_total, axis=2)
    inflow = -jnp.expm1(log_decay_total)
    growth = jnp.exp(cumulative)
    shrink = jnp.exp(-cumulative) * inflow
    length = log_decay_total.shape[2]
    causal = (jnp.arange(length)[:, None] >= jnp.arange(length)[None, :]).astype(jnp.float32)
    intersection = jnp.einsum('bhtd,bhjd->bhtj', queries, keys_in, precision=HIGHEST) * causal
    scores = jnp.einsum('bhtj,bhjs->bhts', intersection, shrink, precision=HIGHEST)
    scores = growth * (scores + jnp.einsum('bhsd,bhtd->bhts', state_key, queries, precision=HIGHEST))
    attend = jax.nn.softmax(scores, axis=-1)
    weighted = attend * growth
    mixing = jnp.einsum('bhts,bhjs->bhtj', weighted, shrink, precision=HIGHEST) * causal
    output = jnp.einsum('bhtj,bhjd->bhtd', mixing, values, precision=HIGHEST)
    output = output + jnp.einsum('bhts,bhsd->bhtd', weighted, state_value, precision=HIGHEST)
    ending = jnp.exp(cumulative[:, :, -1, :])
    remain = ending[:, :, None, :] * shrink
    state_key = ending[..., None] * state_key + jnp.einsum('bhjs,bhjd->bhsd', remain, keys_in, precision=HIGHEST)
    state_value = ending[..., None] * state_value + jnp.einsum('bhjs,bhjd->bhsd', remain, values, precision=HIGHEST)
    return ((state_key, state_value), output)

def recurrence(queries, keys_in, values, log_decay_total, state):
    batch_size, head_count, length = (queries.shape[0], queries.shape[1], queries.shape[2])
    blocks = length // SPAN

    def arrange(array):
        shaped = array.reshape(batch_size, head_count, blocks, SPAN, array.shape[3])
        return jnp.moveaxis(shaped, 2, 0)
    ignored, output = lax.scan(span_pass, state, (arrange(queries), arrange(keys_in), arrange(values), arrange(log_decay_total)))
    return jnp.moveaxis(output, 0, 2).reshape(batch_size, head_count, length, output.shape[-1])

def reference(tokens, input_norm_gain, query_key_value_weight, forget_gate_weight, convolution_filter_taps, slot_forget_rate, extra_forget_log, head_norm_gain, output_projection_weight, feedforward_norm_gain, up_projection_weight, down_projection_weight):
    batch_size, length, width = tokens.shape
    head_count, slot_count = slot_forget_rate.shape
    head_size = head_norm_gain.shape[1]
    normed = normalize(tokens.astype(jnp.float32), input_norm_gain).astype(jnp.bfloat16)
    projected = jnp.dot(normed, query_key_value_weight.reshape(width, 3 * head_count * head_size), preferred_element_type=jnp.float32).astype(jnp.bfloat16)
    padded = jnp.pad(projected.astype(jnp.float32), ((0, 0), (3, 3), (0, 0)))
    taps = convolution_filter_taps.reshape(2, 4, 3 * head_count * head_size)
    gate_scores = jnp.dot(normed, forget_gate_weight, preferred_element_type=jnp.float32)
    log_decay_total = log_decay_values(gate_scores, slot_forget_rate, extra_forget_log)
    zero_state = (jnp.zeros((batch_size, head_count, slot_count, head_size), jnp.float32), jnp.zeros((batch_size, head_count, slot_count, head_size), jnp.float32))
    forward_parts = split_heads(convolve(padded, taps[0], False), head_count, head_size)
    forward_out = recurrence(forward_parts[0], forward_parts[1], forward_parts[2], log_decay_total, zero_state)
    reverse_parts = [flipped(member) for member in split_heads(convolve(padded, taps[1], True), head_count, head_size)]
    reverse_out = flipped(recurrence(reverse_parts[0], reverse_parts[1], reverse_parts[2], flipped(log_decay_total), zero_state))
    gain_shape = head_norm_gain[None, :, None, :]
    combined = normalize(forward_out, gain_shape) + normalize(reverse_out, gain_shape)
    attention = jnp.transpose(combined, (0, 2, 1, 3)).reshape(batch_size, length, head_count * head_size).astype(jnp.bfloat16)
    residual = (tokens.astype(jnp.float32) + jnp.dot(attention, output_projection_weight, preferred_element_type=jnp.float32)).astype(jnp.bfloat16)
    mlp_in = normalize(residual.astype(jnp.float32), feedforward_norm_gain).astype(jnp.bfloat16)
    hidden = jax.nn.gelu(jnp.dot(mlp_in, up_projection_weight, preferred_element_type=jnp.float32)).astype(jnp.bfloat16)
    return (residual.astype(jnp.float32) + jnp.dot(hidden, down_projection_weight, preferred_element_type=jnp.float32)).astype(jnp.bfloat16)
```

```python
import functools

import jax
import jax.numpy as jnp
from jax import lax
from jax.experimental import pallas as pl
from jax.experimental.pallas import tpu as pltpu
from jax.sharding import PartitionSpec as P

SPAN = 64
HALO = 16
EPSILON = 1e-06
MESH = pl.DeviceIdType.MESH
F32 = jnp.float32
BF16 = jnp.bfloat16


def mm(a, b, ca=1, cb=0):
    return lax.dot_general(a, b, (((ca,), (cb,)), ((), ())), preferred_element_type=F32)


def split_mm(ones, values, count):
    total, rest = None, values
    for _ in range(count):
        part = rest.astype(BF16)
        rest = rest - part.astype(F32)
        term = mm(ones, part)
        total = term if total is None else total + term
    return total


def mm_split(values, ones, count):
    total, rest = None, values
    for _ in range(count):
        part = rest.astype(BF16)
        rest = rest - part.astype(F32)
        term = mm(part, ones)
        total = term if total is None else total + term
    return total


def one_minus_exp(x):
    series = 1.0 + x * (1 / 2 + x * (1 / 6 + x * (1 / 24 + x * (1 / 120 + x * (1 / 720)))))
    return jnp.where(x > -0.25, -x * series, 1.0 - jnp.exp(x))


def iota(shape, dim):
    return lax.broadcasted_iota(jnp.int32, shape, dim)


class Gather:
    def __init__(self, hx, nh, seq, block, send, recv):
        self.hx, self.seq, self.block, self.send, self.recv = hx, seq, block, send, recv
        self.masks = []
        m = nh // 2
        while m:
            self.masks.append(m)
            m //= 2
        self.nh = nh
        self.got = {0}

    def copy(self, o, m):
        ref = self.block(self.hx(o))
        return pltpu.make_async_remote_copy(
            src_ref=ref,
            dst_ref=ref,
            send_sem=self.send.at[o ^ m],
            recv_sem=self.recv.at[o ^ m],
            device_id=(self.seq, self.hx(m)),
            device_id_type=MESH,
        )

    def arrive(self, o):
        if o not in self.got:
            ref = self.block(self.hx(o))
            pltpu.make_async_remote_copy(
                src_ref=ref,
                dst_ref=ref,
                send_sem=self.send.at[o],
                recv_sem=self.recv.at[o],
                device_id=(self.seq, self.hx(1)),
                device_id_type=MESH,
            ).wait_recv()
            self.got.add(o)

    def start(self):
        for m in self.masks:
            self.copy(0, m).start()

    def forward(self):
        have = [0]
        for m in self.masks:
            for o in have:
                if o:
                    self.arrive(o)
                    self.copy(o, m).start()
            have = have + [o ^ m for o in have]

    def finish(self):
        for o in range(1, self.nh):
            self.arrive(o)

    def drain(self):
        have = [0]
        for m in self.masks:
            for o in have:
                self.copy(o, m).wait_send()
            have = have + [o ^ m for o in have]


def kernel(
    n,
    nh,
    tok,
    gain1,
    wqkv,
    wgate,
    taps,
    rate,
    extra,
    hgain,
    wo,
    gain2,
    wup,
    wdown,
    out,
    xg,
    wq_v,
    wg_v,
    wo_v,
    up_v,
    dn_v,
    nb,
    pj,
    qkv,
    growth_v,
    shrink_v,
    score_v,
    local_v,
    before_v,
    apost,
    arecv,
    fpost,
    frecv,
    cin,
    csend,
    crecv,
    pair_v,
    pairf_v,
    ag,
    res,
    pf,
    pb,
    rb,
    lsem,
    tok_s,
    tok_r,
    halo_s,
    halo_r,
    wo_s,
    wo_r,
    sib_s,
    sib_r,
    ch_s,
    ch_r,
    at_s,
    at_r,
    rs_s,
    rs_r,
):
    batch, rows, width = tok.shape
    heads, hd = hgain.shape
    spans = rows // SPAN
    s = lax.axis_index("seq")
    h = lax.axis_index("head")

    def hx(o):
        r, bit = h, 1
        while bit <= o:
            if o & bit:
                r = r + bit - 2 * bit * lax.rem(lax.div(r, bit), 2)
            bit *= 2
        return r

    def ring(d):
        return lax.rem(s + d + n, n)

    odd = lax.rem(s, 2)
    pair = lax.div(s, 2)
    pairs = n // 2
    sibling = s + 1 - 2 * odd

    loads = [
        pltpu.make_async_copy(wqkv, wq_v, lsem.at[0]),
        pltpu.make_async_copy(wgate, wg_v, lsem.at[1]),
        pltpu.make_async_copy(wo, wo_v.at[h], lsem.at[2]),
        pltpu.make_async_copy(wup, up_v, lsem.at[3]),
        pltpu.make_async_copy(wdown, dn_v, lsem.at[4]),
    ]
    for load in loads:
        load.start()

    barrier = pltpu.get_barrier_semaphore()
    greeted = [(s, hx(1 << i)) for i in range(nh.bit_length() - 1)]
    greeted += [(ring(d), hx(o)) for d in (-1, 1) for o in range(nh)]
    greeted += [(ring(d), h) for d in (-2, 2)]
    for device in greeted:
        pl.semaphore_signal(barrier, inc=1, device_id=device, device_id_type=MESH)
    xg[h, :, HALO : HALO + rows, :] = tok[...]
    cin[...] = jnp.zeros_like(cin)
    pl.semaphore_wait(barrier, len(greeted))

    tokens = Gather(hx, nh, s, lambda i: xg.at[i, :, HALO : HALO + rows, :], tok_s, tok_r)
    tokens.start()
    halos = []
    for o in range(nh):
        for side in (0, 1):
            src = xg.at[h, :, rows : rows + HALO, :] if side == 0 else xg.at[h, :, HALO : 2 * HALO, :]
            at = 0 if side == 0 else HALO + rows
            halos.append(
                pltpu.make_async_remote_copy(
                    src_ref=src,
                    dst_ref=xg.at[h, :, at : at + HALO, :],
                    send_sem=halo_s.at[side, o],
                    recv_sem=halo_r.at[side, o],
                    device_id=(ring(1) if side == 0 else ring(-1), hx(o)),
                    device_id_type=MESH,
                )
            )
    for copy in halos:
        copy.start()
    tokens.forward()
    projection = Gather(hx, nh, s, lambda i: wo_v.at[i], wo_s, wo_r)
    loads[2].wait()
    projection.start()
    tokens.finish()
    for copy in halos:
        copy.wait_recv()

    tall = rows + 2 * HALO
    row_at = iota((tall, 1), 0)
    inside = jnp.logical_and(
        jnp.logical_or(row_at >= HALO, s > 0),
        jnp.logical_or(row_at < HALO + rows, s < n - 1),
    )
    for b in range(batch):
        parts = [xg[j, b].astype(F32) for j in range(nh)]
        square = parts[0] * parts[0]
        for part in parts[1:]:
            square = square + part * part
        mean = jnp.sum(square, axis=1, keepdims=True) / (nh * width)
        scale = jnp.where(inside, lax.rsqrt(mean + EPSILON), 0.0)
        for j in range(nh):
            cols = slice(j * width, (j + 1) * width)
            nb[b, :, cols] = (parts[j] * scale * gain1[:, cols]).astype(BF16)

    loads[0].wait()
    loads[1].wait()
    normed = nb[...].reshape(batch * tall, nh * width)
    for i in range(3):
        made = mm(normed, wq_v[i]).astype(BF16).astype(F32)
        pj[i] = made.reshape(batch, tall, width)

    lanes = iota((1, width), 1)
    lane_head = lax.div(lanes, hd)
    block_mask = (
        lax.div(iota((width, width), 0), hd) == lax.div(iota((width, width), 1), hd)
    ).astype(F32).astype(BF16)
    causal_t = iota((SPAN, width), 0)
    causal_j = lax.rem(iota((SPAN, width), 1), SPAN)
    causal = [(causal_t >= causal_j).astype(F32), (causal_t <= causal_j).astype(F32)]
    big_t, big_j = iota((rows, rows), 0), iota((rows, rows), 1)
    same = lax.div(big_t, SPAN) == lax.div(big_j, SPAN)
    running = [
        jnp.logical_and(same, big_t >= big_j).astype(F32).astype(BF16),
        jnp.logical_and(same, big_t <= big_j).astype(F32).astype(BF16),
    ]
    rate_row = jnp.concatenate([rate[i : i + 1, :] for i in range(heads)], axis=1)
    gain_row = jnp.concatenate([hgain[i : i + 1, :] for i in range(heads)], axis=1)

    def expand(x):
        return jnp.concatenate([x] * heads, axis=0) * block_mask

    def compact(x):
        total = None
        for i in range(heads):
            term = jnp.where(lane_head == i, x[i * hd : (i + 1) * hd], 0.0)
            total = term if total is None else total + term
        return total

    decays = []
    for b in range(batch):
        logits = mm(nb[b, HALO : HALO + rows, :], wg_v[...])
        column = jnp.sum(
            jnp.where(big_t == big_j, extra[b : b + 1, :], 0.0), axis=1, keepdims=True
        )
        decays.append(-2.0 * rate_row * jax.nn.sigmoid(logits) - column)

    def sib_copies(d):
        return [
            pltpu.make_async_remote_copy(
                src_ref=src.at[d],
                dst_ref=dst.at[d],
                send_sem=sib_s.at[d, k],
                recv_sem=sib_r.at[d, k],
                device_id=(sibling, h),
                device_id_type=MESH,
            )
            for k, (src, dst) in enumerate(((apost, arecv), (fpost, frecv)))
        ]

    fpost[...] = jnp.zeros_like(fpost)
    order = [list(range(spans)), list(range(spans))[::-1]]
    for d in (0, 1):
        for b in range(batch):
            for i in range(3):
                acc = None
                for j in range(4):
                    first = HALO + j if d else HALO - j
                    term = taps[d, i, j : j + 1, :] * pj[i, b, first : first + rows, :]
                    acc = term if acc is None else acc + term
                qkv[d, i, b] = (acc * jax.nn.sigmoid(acc)).astype(BF16)
            ld = decays[b]
            inflow = one_minus_exp(ld)
            cum = split_mm(running[d], ld, 3)
            growth_v[d, b] = jnp.exp(cum)
            shrink_v[d, b] = (jnp.exp(-cum) * inflow).astype(BF16)
            state = jnp.zeros((2 * hd, width), F32)
            past = jnp.zeros((1, width), F32)
            for g in order[d]:
                r0 = g * SPAN
                local_v[d, b, g] = state
                before_v[d, b, g : g + 1, :] = jnp.exp(past)
                last = r0 if d else r0 + SPAN - 1
                total = cum[last : last + 1, :]
                remain = (jnp.exp(total - cum[r0 : r0 + SPAN]) * inflow[r0 : r0 + SPAN]).astype(BF16)
                new = [
                    compact(mm(qkv[d, i, b, r0 : r0 + SPAN, :], remain, 0, 0)) for i in (1, 2)
                ]
                state = jnp.exp(total) * state + jnp.concatenate(new, axis=0)
                past = past + total
            apost[d, b] = state.astype(BF16)
            fpost[d, b : b + 1, :] = jnp.exp(past)
        for copy in sib_copies(d):
            copy.start()

    projection.forward()

    def local_scores(d):
        for b in range(batch):
            for g in range(spans):
                span = slice(g * SPAN, (g + 1) * SPAN)
                inter = mm(qkv[d, 0, b, span, :], expand(qkv[d, 1, b, span, :]), 1, 1) * causal[d]
                score_v[d, b, span, :] = mm(inter.astype(BF16), expand(shrink_v[d, b, span, :]))

    local_scores(0)

    later = [odd.astype(F32), 1.0 - odd.astype(F32)]
    for d in (0, 1):
        for copy in sib_copies(d):
            copy.wait_recv()
        for b in range(batch):
            mine, other = apost[d, b].astype(F32), arecv[d, b].astype(F32)
            fm, fo = fpost[d, b : b + 1, :], frecv[d, b : b + 1, :]
            pair_v[d, b] = later[d] * (fm * other + mine) + (1.0 - later[d]) * (fo * mine + other)
            pairf_v[d, b : b + 1, :] = fm * fo

    has_in = [pair > 0, pair < pairs - 1]
    has_out = [pair < pairs - 1, pair > 0]

    def hop_copy(d, b):
        return pltpu.make_async_remote_copy(
            src_ref=csend.at[d, b],
            dst_ref=crecv.at[d, b],
            send_sem=ch_s.at[d, b],
            recv_sem=ch_r.at[d, b],
            device_id=(ring(-2) if d else ring(2), h),
            device_id_type=MESH,
        )

    def hop(d):
        for b in range(batch):

            @pl.when(has_in[d])
            def _():
                hop_copy(d, b).wait_recv()
                cin[d, b] = crecv[d, b].astype(F32)

            @pl.when(has_out[d])
            def _():
                csend[d, b] = (pairf_v[d, b : b + 1, :] * cin[d, b] + pair_v[d, b]).astype(BF16)
                hop_copy(d, b).start()

    @pl.when(2 * pair < pairs)
    def _():
        hop(0)
        hop(1)

    @pl.when(2 * pair >= pairs)
    def _():
        hop(1)
        hop(0)

    local_scores(1)

    attends = [
        Gather(hx, nh, s, lambda i, b=b: ag.at[i, b], at_s.at[b], at_r.at[b]) for b in range(batch)
    ]
    for b in range(batch):
        for g in range(spans):
            span = slice(g * SPAN, (g + 1) * SPAN)
            combined = jnp.zeros((SPAN, width), F32)
            for d in (0, 1):
                fo = frecv[d, b : b + 1, :]
                carry = cin[d, b]
                entry = later[d] * (fo * carry + arecv[d, b].astype(F32)) + (1.0 - later[d]) * carry
                state = (before_v[d, b, g : g + 1, :] * entry + local_v[d, b, g]).astype(BF16)
                growth = growth_v[d, b, span, :]
                scores = score_v[d, b, span, :] + mm(qkv[d, 0, b, span, :], expand(state[:hd]))
                scores = growth * scores
                top = None
                for i in range(heads):
                    best = jnp.max(
                        jnp.where(lane_head == i, scores, -jnp.inf), axis=1, keepdims=True
                    )
                    top = best if top is None else jnp.where(lane_head == i, best, top)
                power = jnp.exp(scores - top)
                norm = mm_split(power, block_mask, 2)
                weighted = (power / norm * growth).astype(BF16)
                mixing = mm(weighted, expand(shrink_v[d, b, span, :]), 1, 1) * causal[d]
                made = mm(mixing.astype(BF16), expand(qkv[d, 2, b, span, :]))
                made = made + mm(weighted, expand(state[hd:]), 1, 1)
                mean = mm_split(made * made, block_mask, 2) / hd
                combined = combined + made * lax.rsqrt(mean + EPSILON) * gain_row
            ag[h, b, span, :] = combined.astype(BF16)
        attends[b].start()
        if b:
            attends[b - 1].forward()
    attends[batch - 1].forward()

    projection.finish()
    loads[3].wait()
    loads[4].wait()

    masks = [1 << i for i in range(nh.bit_length() - 1)]

    def rs_copy(b, o, m):
        return pltpu.make_async_remote_copy(
            src_ref=pb.at[hx(o), b],
            dst_ref=rb.at[o ^ m, m.bit_length() - 1, b],
            send_sem=rs_s.at[b, o],
            recv_sem=rs_r.at[b, o],
            device_id=(s, hx(m)),
            device_id_type=MESH,
        )

    def live(k):
        return [o for o in range(nh) if o % masks[k] == 0]

    def rs_send(b, k):
        m = masks[k]
        for o in live(k):
            if o & m:
                pb[hx(o), b] = pf[hx(o), b].astype(BF16)
                rs_copy(b, o, m).start()

    def rs_take(b, k):
        m = masks[k]
        for o in live(k):
            if o & m:
                rs_copy(b, o, m).wait_recv()
                kept = hx(o ^ m)
                pf[kept, b] = pf[kept, b] + rb[o ^ m, k, b].astype(F32)

    wo_all = wo_v[...].reshape(nh * width, nh * width)
    for b in range(batch):
        attends[b].finish()
        attention = jnp.concatenate([ag[j, b] for j in range(nh)], axis=1)
        whole = jnp.concatenate([xg[j, b, HALO : HALO + rows, :] for j in range(nh)], axis=1)
        residual = (whole.astype(F32) + mm(attention, wo_all)).astype(BF16)
        wide = residual.astype(F32)
        for j in range(nh):
            res[j, b] = residual[:, j * width : (j + 1) * width]
        mean = jnp.mean(wide * wide, axis=1, keepdims=True)
        mlp_in = (wide * lax.rsqrt(mean + EPSILON) * gain2[...]).astype(BF16)
        hidden = jax.nn.gelu(mm(mlp_in, up_v[...])).astype(BF16)
        for j in range(nh):
            pf[j, b] = mm(hidden, dn_v[:, j * width : (j + 1) * width])
        rs_send(b, 0)
    for k in range(len(masks)):
        for b in range(batch):
            rs_take(b, k)
            if k + 1 < len(masks):
                rs_send(b, k + 1)
    for b in range(batch):
        out[b] = (res[h, b].astype(F32) + pf[h, b]).astype(BF16)

    tokens.drain()
    projection.drain()
    for copy in halos:
        copy.wait_send()
    for d in (0, 1):
        for copy in sib_copies(d):
            copy.wait_send()

        @pl.when(has_out[d])
        def _():
            for b in range(batch):
                hop_copy(d, b).wait_send()

    for b in range(batch):
        attends[b].drain()
        for k, m in enumerate(masks):
            for o in live(k):
                if o & m:
                    rs_copy(b, o, m).wait_send()


def local(
    n,
    nh,
    tokens,
    input_norm_gain,
    query_key_value_weight,
    forget_gate_weight,
    convolution_filter_taps,
    slot_forget_rate,
    extra_forget_log,
    head_norm_gain,
    output_projection_weight,
    feedforward_norm_gain,
    up_projection_weight,
    down_projection_weight,
):
    batch, rows, width = tokens.shape
    depth = nh * width
    hidden = up_projection_weight.shape[1]
    spans = rows // SPAN
    hd = head_norm_gain.shape[1]
    tall = rows + 2 * HALO
    vmem = pl.BlockSpec(memory_space=pltpu.VMEM)
    anywhere = pl.BlockSpec(memory_space=pl.ANY)
    dma = pltpu.SemaphoreType.DMA
    bits = nh.bit_length() - 1
    scratch = [
        pltpu.VMEM((nh, batch, tall, width), BF16),
        pltpu.VMEM((3, depth, width), BF16),
        pltpu.VMEM((depth, width), BF16),
        pltpu.VMEM((nh, width, depth), BF16),
        pltpu.VMEM((depth, hidden), BF16),
        pltpu.VMEM((hidden, depth), BF16),
        pltpu.VMEM((batch, tall, depth), BF16),
        pltpu.VMEM((3, batch, tall, width), F32),
        pltpu.VMEM((2, 3, batch, rows, width), BF16),
        pltpu.VMEM((2, batch, rows, width), F32),
        pltpu.VMEM((2, batch, rows, width), BF16),
        pltpu.VMEM((2, batch, rows, width), F32),
        pltpu.VMEM((2, batch, spans, 2 * hd, width), F32),
        pltpu.VMEM((2, batch, spans, width), F32),
        pltpu.VMEM((2, batch, 2 * hd, width), BF16),
        pltpu.VMEM((2, batch, 2 * hd, width), BF16),
        pltpu.VMEM((2, 8 * pl.cdiv(batch, 8), width), F32),
        pltpu.VMEM((2, 8 * pl.cdiv(batch, 8), width), F32),
        pltpu.VMEM((2, batch, 2 * hd, width), F32),
        pltpu.VMEM((2, batch, 2 * hd, width), BF16),
        pltpu.VMEM((2, batch, 2 * hd, width), BF16),
        pltpu.VMEM((2, batch, 2 * hd, width), F32),
        pltpu.VMEM((2, batch, width), F32),
        pltpu.VMEM((nh, batch, rows, width), BF16),
        pltpu.VMEM((nh, batch, rows, width), BF16),
        pltpu.VMEM((nh, batch, rows, width), F32),
        pltpu.VMEM((nh, batch, rows, width), BF16),
        pltpu.VMEM((nh, bits, batch, rows, width), BF16),
        dma((5,)),
        dma((nh,)),
        dma((nh,)),
        dma((2, nh)),
        dma((2, nh)),
        dma((nh,)),
        dma((nh,)),
        dma((2, 2)),
        dma((2, 2)),
        dma((2, batch)),
        dma((2, batch)),
        dma((batch, nh)),
        dma((batch, nh)),
        dma((batch, nh)),
        dma((batch, nh)),
    ]
    return pl.pallas_call(
        functools.partial(kernel, n, nh),
        out_shape=jax.ShapeDtypeStruct(tokens.shape, tokens.dtype),
        in_specs=[
            vmem,
            vmem,
            anywhere,
            anywhere,
            vmem,
            vmem,
            vmem,
            vmem,
            anywhere,
            vmem,
            anywhere,
            anywhere,
        ],
        out_specs=vmem,
        scratch_shapes=scratch,
        compiler_params=pltpu.CompilerParams(
            collective_id=0, has_side_effects=True, vmem_limit_bytes=56 * 2**20
        ),
        name="layer",
    )(
        tokens,
        input_norm_gain.reshape(1, -1),
        jnp.transpose(query_key_value_weight, (1, 0, 2)),
        forget_gate_weight,
        jnp.transpose(convolution_filter_taps, (0, 2, 1, 3)),
        slot_forget_rate,
        extra_forget_log,
        head_norm_gain,
        output_projection_weight,
        feedforward_norm_gain.reshape(1, -1),
        up_projection_weight,
        down_projection_weight,
    )


def solution(mesh):
    in_specs = (
        P(None, "seq", "head"),
        P(),
        P(None, None, "head"),
        P(None, "head"),
        P(None, None, None, "head"),
        P("head", None),
        P(None, "seq"),
        P("head", None),
        P("head", None),
        P(),
        P(None, "head"),
        P("head", None),
    )
    out_specs = P(None, "seq", "head")
    return jax.shard_map(
        functools.partial(local, mesh.shape["seq"], mesh.shape["head"]),
        mesh=mesh,
        in_specs=in_specs,
        out_specs=out_specs,
        check_vma=False,
    )
```

```python
import functools

import jax
import jax.numpy as jnp
from jax import lax
from jax.experimental import pallas as pl
from jax.experimental.pallas import tpu as pltpu
from jax.sharding import PartitionSpec as P

SPAN = 64
HALO = 16
EPSILON = 1e-06
MESH = pl.DeviceIdType.MESH
F32 = jnp.float32
BF16 = jnp.bfloat16


def mm(a, b, ca=1, cb=0):
    return lax.dot_general(a, b, (((ca,), (cb,)), ((), ())), preferred_element_type=F32)


def split_mm(ones, values, count):
    total, rest = None, values
    for _ in range(count):
        part = rest.astype(BF16)
        rest = rest - part.astype(F32)
        term = mm(ones, part)
        total = term if total is None else total + term
    return total


def mm_split(values, ones, count):
    total, rest = None, values
    for _ in range(count):
        part = rest.astype(BF16)
        rest = rest - part.astype(F32)
        term = mm(part, ones)
        total = term if total is None else total + term
    return total


def one_minus_exp(x):
    series = 1.0 + x * (1 / 2 + x * (1 / 6 + x * (1 / 24 + x * (1 / 120 + x * (1 / 720)))))
    return jnp.where(x > -0.25, -x * series, 1.0 - jnp.exp(x))


def iota(shape, dim):
    return lax.broadcasted_iota(jnp.int32, shape, dim)


class Gather:
    def __init__(self, hx, nh, seq, block, send, recv):
        self.hx, self.seq, self.block, self.send, self.recv = hx, seq, block, send, recv
        self.masks = []
        m = nh // 2
        while m:
            self.masks.append(m)
            m //= 2
        self.nh = nh
        self.got = {0}

    def copy(self, o, m):
        ref = self.block(self.hx(o))
        return pltpu.make_async_remote_copy(
            src_ref=ref,
            dst_ref=ref,
            send_sem=self.send.at[o ^ m],
            recv_sem=self.recv.at[o ^ m],
            device_id=(self.seq, self.hx(m)),
            device_id_type=MESH,
        )

    def arrive(self, o):
        if o not in self.got:
            ref = self.block(self.hx(o))
            pltpu.make_async_remote_copy(
                src_ref=ref,
                dst_ref=ref,
                send_sem=self.send.at[o],
                recv_sem=self.recv.at[o],
                device_id=(self.seq, self.hx(1)),
                device_id_type=MESH,
            ).wait_recv()
            self.got.add(o)

    def start(self):
        for m in self.masks:
            self.copy(0, m).start()

    def forward(self):
        have = [0]
        for m in self.masks:
            for o in have:
                if o:
                    self.arrive(o)
                    self.copy(o, m).start()
            have = have + [o ^ m for o in have]

    def finish(self):
        for o in range(1, self.nh):
            self.arrive(o)

    def drain(self):
        have = [0]
        for m in self.masks:
            for o in have:
                self.copy(o, m).wait_send()
            have = have + [o ^ m for o in have]


def kernel(
    n,
    nh,
    tok,
    gain1,
    wqkv,
    wgate,
    taps,
    rate,
    extra,
    hgain,
    wo,
    gain2,
    wup,
    wdown,
    out,
    xg,
    wq_v,
    wg_v,
    wo_v,
    up_v,
    dn_v,
    nb,
    pj,
    qkv,
    growth_v,
    shrink_v,
    score_v,
    local_v,
    before_v,
    apost,
    arecv,
    fpost,
    frecv,
    cin,
    csend,
    crecv,
    sst,
    begin,
    pair_v,
    pairf_v,
    ag,
    res,
    pf,
    pb,
    rb,
    lsem,
    tok_s,
    tok_r,
    halo_s,
    halo_r,
    wo_s,
    wo_r,
    sib_s,
    sib_r,
    ch_s,
    ch_r,
    st_s,
    st_r,
    at_s,
    at_r,
    rs_s,
    rs_r,
):
    batch, rows, width = tok.shape
    heads, hd = hgain.shape
    spans = rows // SPAN
    s = lax.axis_index("seq")
    h = lax.axis_index("head")

    def hx(o):
        r, bit = h, 1
        while bit <= o:
            if o & bit:
                r = r + bit - 2 * bit * lax.rem(lax.div(r, bit), 2)
            bit *= 2
        return r

    def ring(d):
        return lax.rem(s + d + n, n)

    odd = lax.rem(s, 2)
    pair = lax.div(s, 2)
    pairs = n // 2
    sibling = s + 1 - 2 * odd

    loads = [
        pltpu.make_async_copy(wqkv, wq_v, lsem.at[0]),
        pltpu.make_async_copy(wgate, wg_v, lsem.at[1]),
        pltpu.make_async_copy(wo, wo_v.at[h], lsem.at[2]),
        pltpu.make_async_copy(wup, up_v, lsem.at[3]),
        pltpu.make_async_copy(wdown, dn_v, lsem.at[4]),
    ]
    for load in loads:
        load.start()

    barrier = pltpu.get_barrier_semaphore()
    greeted = [(s, hx(1 << i)) for i in range(nh.bit_length() - 1)]
    greeted += [(ring(d), hx(o)) for d in (-1, 1) for o in range(nh)]
    greeted += [(ring(d), h) for d in (-2, 2)]
    for device in greeted:
        pl.semaphore_signal(barrier, inc=1, device_id=device, device_id_type=MESH)
    xg[h, :, HALO : HALO + rows, :] = tok[...]
    cin[...] = jnp.zeros_like(cin)
    pl.semaphore_wait(barrier, len(greeted))

    tokens = Gather(hx, nh, s, lambda i: xg.at[i, :, HALO : HALO + rows, :], tok_s, tok_r)
    tokens.start()
    halos = []
    for o in range(nh):
        for side in (0, 1):
            src = xg.at[h, :, rows : rows + HALO, :] if side == 0 else xg.at[h, :, HALO : 2 * HALO, :]
            at = 0 if side == 0 else HALO + rows
            halos.append(
                pltpu.make_async_remote_copy(
                    src_ref=src,
                    dst_ref=xg.at[h, :, at : at + HALO, :],
                    send_sem=halo_s.at[side, o],
                    recv_sem=halo_r.at[side, o],
                    device_id=(ring(1) if side == 0 else ring(-1), hx(o)),
                    device_id_type=MESH,
                )
            )
    for copy in halos:
        copy.start()
    tokens.forward()
    projection = Gather(hx, nh, s, lambda i: wo_v.at[i], wo_s, wo_r)
    loads[2].wait()
    projection.start()
    tokens.finish()
    for copy in halos:
        copy.wait_recv()

    tall = rows + 2 * HALO
    row_at = iota((tall, 1), 0)
    inside = jnp.logical_and(
        jnp.logical_or(row_at >= HALO, s > 0),
        jnp.logical_or(row_at < HALO + rows, s < n - 1),
    )
    for b in range(batch):
        parts = [xg[j, b].astype(F32) for j in range(nh)]
        square = parts[0] * parts[0]
        for part in parts[1:]:
            square = square + part * part
        mean = jnp.sum(square, axis=1, keepdims=True) / (nh * width)
        scale = jnp.where(inside, lax.rsqrt(mean + EPSILON), 0.0)
        for j in range(nh):
            cols = slice(j * width, (j + 1) * width)
            nb[b, :, cols] = (parts[j] * scale * gain1[:, cols]).astype(BF16)

    loads[0].wait()
    loads[1].wait()
    normed = nb[...].reshape(batch * tall, nh * width)

    def project(i):
        made = mm(normed, wq_v[i]).astype(BF16).astype(F32)
        pj[i] = made.reshape(batch, tall, width)

    def convolve(d, i, b):
        acc = None
        for j in range(4):
            first = HALO + j if d else HALO - j
            term = taps[d, i, j : j + 1, :] * pj[i, b, first : first + rows, :]
            acc = term if acc is None else acc + term
        qkv[d, i, b] = (acc * jax.nn.sigmoid(acc)).astype(BF16)

    project(1)
    project(2)

    lanes = iota((1, width), 1)
    lane_head = lax.div(lanes, hd)
    block_mask = (
        lax.div(iota((width, width), 0), hd) == lax.div(iota((width, width), 1), hd)
    ).astype(F32).astype(BF16)
    causal_t = iota((SPAN, width), 0)
    causal_j = lax.rem(iota((SPAN, width), 1), SPAN)
    causal = [(causal_t >= causal_j).astype(F32), (causal_t <= causal_j).astype(F32)]
    big_t, big_j = iota((rows, rows), 0), iota((rows, rows), 1)
    same = lax.div(big_t, SPAN) == lax.div(big_j, SPAN)
    running = [
        jnp.logical_and(same, big_t >= big_j).astype(F32).astype(BF16),
        jnp.logical_and(same, big_t <= big_j).astype(F32).astype(BF16),
    ]
    rate_row = jnp.concatenate([rate[i : i + 1, :] for i in range(heads)], axis=1)
    gain_row = jnp.concatenate([hgain[i : i + 1, :] for i in range(heads)], axis=1)

    def expand(x):
        return jnp.concatenate([x] * heads, axis=0) * block_mask

    def compact(x):
        total = None
        for i in range(heads):
            term = jnp.where(lane_head == i, x[i * hd : (i + 1) * hd], 0.0)
            total = term if total is None else total + term
        return total

    decays = []
    for b in range(batch):
        logits = mm(nb[b, HALO : HALO + rows, :], wg_v[...])
        column = jnp.sum(
            jnp.where(big_t == big_j, extra[b : b + 1, :], 0.0), axis=1, keepdims=True
        )
        decays.append(-2.0 * rate_row * jax.nn.sigmoid(logits) - column)

    def sib_copies(d):
        return [
            pltpu.make_async_remote_copy(
                src_ref=src,
                dst_ref=dst,
                send_sem=sib_s.at[d, k],
                recv_sem=sib_r.at[d, k],
                device_id=(sibling, h),
                device_id_type=MESH,
            )
            for k, (src, dst) in enumerate(
                ((apost.at[d, 1 - odd], arecv.at[d]), (fpost.at[d], frecv.at[d]))
            )
        ]

    fpost[...] = jnp.zeros_like(fpost)
    order = [list(range(spans)), list(range(spans))[::-1]]
    for d in (0, 1):
        for b in range(batch):
            for i in (1, 2):
                convolve(d, i, b)
            ld = decays[b]
            inflow = one_minus_exp(ld)
            cum = split_mm(running[d], ld, 3)
            growth_v[d, b] = jnp.exp(cum)
            shrink_v[d, b] = (jnp.exp(-cum) * inflow).astype(BF16)
            state = jnp.zeros((2 * hd, width), F32)
            past = jnp.zeros((1, width), F32)
            for g in order[d]:
                r0 = g * SPAN
                local_v[d, b, g] = state
                before_v[d, b, g : g + 1, :] = jnp.exp(past)
                last = r0 if d else r0 + SPAN - 1
                total = cum[last : last + 1, :]
                remain = (jnp.exp(total - cum[r0 : r0 + SPAN]) * inflow[r0 : r0 + SPAN]).astype(BF16)
                new = [
                    compact(mm(qkv[d, i, b, r0 : r0 + SPAN, :], remain, 0, 0)) for i in (1, 2)
                ]
                state = jnp.exp(total) * state + jnp.concatenate(new, axis=0)
                past = past + total
            apost[d, 0, b] = state[:hd].astype(BF16)
            apost[d, 1, b] = state[hd:].astype(BF16)
            fpost[d, b : b + 1, :] = jnp.exp(past)
        for copy in sib_copies(d):
            copy.start()

    project(0)
    for d in (0, 1):
        for b in range(batch):
            convolve(d, 0, b)

    def local_scores(d):
        blocks = [(b, slice(g * SPAN, (g + 1) * SPAN)) for b in range(batch) for g in range(spans)]
        inter = [
            mm(qkv[d, 0, b, span, :], expand(qkv[d, 1, b, span, :]), 1, 1) for b, span in blocks
        ]
        inter = [(x * causal[d]).astype(BF16) for x in inter]
        made = [mm(x, expand(shrink_v[d, b, span, :])) for x, (b, span) in zip(inter, blocks)]
        for x, (b, span) in zip(made, blocks):
            score_v[d, b, span, :] = x

    later = [odd.astype(F32), 1.0 - odd.astype(F32)]
    for d in (0, 1):
        for copy in sib_copies(d):
            copy.wait_recv()
        for b in range(batch):
            mine, other = apost[d, odd, b].astype(F32), arecv[d, b].astype(F32)
            fm, fo = fpost[d, b : b + 1, :], frecv[d, b : b + 1, :]
            pair_v[d, b] = later[d] * (fm * other + mine) + (1.0 - later[d]) * (fo * mine + other)
            pairf_v[d, b : b + 1, :] = fm * fo

    first_pair = [pair == 0, pair == pairs - 1]
    last_pair = [pair == pairs - 1, pair == 0]

    def hop_copy(d, b):
        return pltpu.make_async_remote_copy(
            src_ref=csend.at[d, b],
            dst_ref=crecv.at[d, b],
            send_sem=ch_s.at[d, b],
            recv_sem=ch_r.at[d, b],
            device_id=(ring(-2) if d else ring(2), h),
            device_id_type=MESH,
        )

    def start_copy(d, b):
        return pltpu.make_async_remote_copy(
            src_ref=sst.at[d, b],
            dst_ref=begin.at[d, odd, b],
            send_sem=st_s.at[d, b],
            recv_sem=st_r.at[d, b],
            device_id=(sibling, h),
            device_id_type=MESH,
        )

    def await_start(d, b):
        pltpu.make_async_remote_copy(
            src_ref=sst.at[d, b],
            dst_ref=begin.at[d, 1 - odd, b],
            send_sem=st_s.at[d, b],
            recv_sem=st_r.at[d, b],
            device_id=(sibling, h),
            device_id_type=MESH,
        ).wait_recv()

    def pass_on(d, b):
        csend[d, b] = (pairf_v[d, b : b + 1, :] * cin[d, b] + pair_v[d, b]).astype(BF16)
        hop_copy(d, b).start()

    def open_chain(d):
        @pl.when(jnp.logical_and(first_pair[d], jnp.logical_not(last_pair[d])))
        def _():
            for b in range(batch):
                pass_on(d, b)

    def hop(d):
        for b in range(batch):

            @pl.when(jnp.logical_not(first_pair[d]))
            def _():
                hop_copy(d, b).wait_recv()
                cin[d, b] = crecv[d, b].astype(F32)

            @pl.when(jnp.logical_not(jnp.logical_or(first_pair[d], last_pair[d])))
            def _():
                pass_on(d, b)

            carry = cin[d, b]
            fm, fo = fpost[d, b : b + 1, :], frecv[d, b : b + 1, :]
            mine, other = apost[d, odd, b].astype(F32), arecv[d, b].astype(F32)
            theirs = (1.0 - later[d]) * (fm * carry + mine) + later[d] * carry
            sst[d, b] = theirs.astype(BF16)
            start_copy(d, b).start()
            own = later[d] * (fo * carry + other) + (1.0 - later[d]) * carry
            begin[d, odd, b] = own.astype(BF16)

    lower = 2 * pair < pairs
    open_chain(0)
    open_chain(1)
    local_scores(0)

    @pl.when(lower)
    def _():
        hop(0)

    @pl.when(jnp.logical_not(lower))
    def _():
        hop(1)

    local_scores(1)

    @pl.when(lower)
    def _():
        hop(1)

    @pl.when(jnp.logical_not(lower))
    def _():
        hop(0)

    projection.forward()

    attends = [
        Gather(hx, nh, s, lambda i, b=b: ag.at[i, b], at_s.at[b], at_r.at[b]) for b in range(batch)
    ]
    group = min(width, 128)

    def head_max(x):
        tops = []
        for c in range(0, width, group):
            part, head = x[:, c : c + group], lane_head[:, c : c + group]
            top = None
            for i in range(c // hd, (c + group) // hd):
                best = jnp.max(jnp.where(head == i, part, -jnp.inf), axis=1, keepdims=True)
                top = best if top is None else jnp.where(head == i, best, top)
            tops.append(jnp.broadcast_to(top, part.shape))
        return jnp.concatenate(tops, axis=1)

    for b in range(batch):
        for d in (0, 1):
            await_start(d, b)
        blocks = [(d, g, slice(g * SPAN, (g + 1) * SPAN)) for g in range(spans) for d in (0, 1)]
        keys, values = [
            [
                (
                    before_v[d, b, g : g + 1, :] * begin[d, i, b].astype(F32)
                    + local_v[d, b, g, i * hd : (i + 1) * hd, :]
                ).astype(BF16)
                for d, g, span in blocks
            ]
            for i in (0, 1)
        ]
        growth = [growth_v[d, b, span, :] for d, g, span in blocks]
        scores = [mm(qkv[d, 0, b, span, :], expand(k)) for (d, g, span), k in zip(blocks, keys)]
        scores = [
            w * (score_v[d, b, span, :] + x) for (d, g, span), x, w in zip(blocks, scores, growth)
        ]
        power = [jnp.exp(x - head_max(x)) for x in scores]
        norm = [mm(x.astype(BF16), block_mask) for x in power]
        weighted = [(x / y * w).astype(BF16) for x, y, w in zip(power, norm, growth)]
        mixing = [
            mm(x, expand(shrink_v[d, b, span, :]), 1, 1) for (d, g, span), x in zip(blocks, weighted)
        ]
        mixing = [(x * causal[d]).astype(BF16) for (d, g, span), x in zip(blocks, mixing)]
        carried = [mm(x, expand(v), 1, 1) for x, v in zip(weighted, values)]
        made = [
            x + mm(y, expand(qkv[d, 2, b, span, :]))
            for (d, g, span), x, y in zip(blocks, carried, mixing)
        ]
        mean = [mm((x * x).astype(BF16), block_mask) / hd for x in made]
        made = [x * lax.rsqrt(y + EPSILON) * gain_row for x, y in zip(made, mean)]
        for g in range(spans):
            span = slice(g * SPAN, (g + 1) * SPAN)
            ag[h, b, span, :] = (made[2 * g] + made[2 * g + 1]).astype(BF16)
        attends[b].start()
    attends[0].forward()

    projection.finish()
    loads[3].wait()
    loads[4].wait()

    masks = [1 << i for i in range(nh.bit_length() - 1)]

    def rs_copy(b, o, m):
        return pltpu.make_async_remote_copy(
            src_ref=pb.at[hx(o), b],
            dst_ref=rb.at[o ^ m, m.bit_length() - 1, b],
            send_sem=rs_s.at[b, o],
            recv_sem=rs_r.at[b, o],
            device_id=(s, hx(m)),
            device_id_type=MESH,
        )

    leaving = sorted(range(nh), key=lambda o: [-((o >> k) & 1) for k in range(len(masks))])

    def level(o):
        return next((k for k, m in enumerate(masks) if o & m), len(masks))

    def settle(b, o):
        total = pf[hx(o), b]
        for k in range(level(o)):
            rs_copy(b, o ^ masks[k], masks[k]).wait_recv()
            total = total + rb[o, k, b].astype(F32)
        if o:
            pb[hx(o), b] = total.astype(BF16)
            rs_copy(b, o, masks[level(o)]).start()
        else:
            out[b] = (res[h, b].astype(F32) + total).astype(BF16)

    wo_all = wo_v[...].reshape(nh * width, nh * width)
    for b in range(batch):
        attends[b].finish()
        attention = jnp.concatenate([ag[j, b] for j in range(nh)], axis=1)
        whole = jnp.concatenate([xg[j, b, HALO : HALO + rows, :] for j in range(nh)], axis=1)
        residual = (whole.astype(F32) + mm(attention, wo_all)).astype(BF16)
        wide = residual.astype(F32)
        for j in range(nh):
            res[j, b] = residual[:, j * width : (j + 1) * width]
        mean = jnp.mean(wide * wide, axis=1, keepdims=True)
        mlp_in = (wide * lax.rsqrt(mean + EPSILON) * gain2[...]).astype(BF16)
        hidden = jax.nn.gelu(mm(mlp_in, up_v[...])).astype(BF16)
        if b + 1 < batch:
            attends[b + 1].forward()
        if b:
            for o in leaving:
                if 0 < level(o) < len(masks):
                    settle(b - 1, o)
        for o in leaving:
            cols = pl.ds(pl.multiple_of(hx(o) * width, width), width)
            made = mm(hidden, dn_v[:, cols])
            if level(o) == 0 and o:
                pb[hx(o), b] = made.astype(BF16)
                rs_copy(b, o, masks[0]).start()
            else:
                pf[hx(o), b] = made
                if o and b == batch - 1:
                    settle(b, o)
    for b in range(batch):
        settle(b, 0)

    tokens.drain()
    projection.drain()
    for copy in halos:
        copy.wait_send()
    for d in (0, 1):
        for copy in sib_copies(d):
            copy.wait_send()

        @pl.when(jnp.logical_not(last_pair[d]))
        def _():
            for b in range(batch):
                hop_copy(d, b).wait_send()

        for b in range(batch):
            start_copy(d, b).wait_send()

    for b in range(batch):
        attends[b].drain()
        for o in range(1, nh):
            rs_copy(b, o, masks[level(o)]).wait_send()


def local(
    n,
    nh,
    tokens,
    input_norm_gain,
    query_key_value_weight,
    forget_gate_weight,
    convolution_filter_taps,
    slot_forget_rate,
    extra_forget_log,
    head_norm_gain,
    output_projection_weight,
    feedforward_norm_gain,
    up_projection_weight,
    down_projection_weight,
):
    batch, rows, width = tokens.shape
    depth = nh * width
    hidden = up_projection_weight.shape[1]
    spans = rows // SPAN
    hd = head_norm_gain.shape[1]
    tall = rows + 2 * HALO
    vmem = pl.BlockSpec(memory_space=pltpu.VMEM)
    anywhere = pl.BlockSpec(memory_space=pl.ANY)
    dma = pltpu.SemaphoreType.DMA
    bits = nh.bit_length() - 1
    scratch = [
        pltpu.VMEM((nh, batch, tall, width), BF16),
        pltpu.VMEM((3, depth, width), BF16),
        pltpu.VMEM((depth, width), BF16),
        pltpu.VMEM((nh, width, depth), BF16),
        pltpu.VMEM((depth, hidden), BF16),
        pltpu.VMEM((hidden, depth), BF16),
        pltpu.VMEM((batch, tall, depth), BF16),
        pltpu.VMEM((3, batch, tall, width), F32),
        pltpu.VMEM((2, 3, batch, rows, width), BF16),
        pltpu.VMEM((2, batch, rows, width), F32),
        pltpu.VMEM((2, batch, rows, width), BF16),
        pltpu.VMEM((2, batch, rows, width), F32),
        pltpu.VMEM((2, batch, spans, 2 * hd, width), F32),
        pltpu.VMEM((2, batch, spans, width), F32),
        pltpu.VMEM((2, 2, batch, hd, width), BF16),
        pltpu.VMEM((2, batch, hd, width), BF16),
        pltpu.VMEM((2, 8 * pl.cdiv(batch, 8), width), F32),
        pltpu.VMEM((2, 8 * pl.cdiv(batch, 8), width), F32),
        pltpu.VMEM((2, batch, hd, width), F32),
        pltpu.VMEM((2, batch, hd, width), BF16),
        pltpu.VMEM((2, batch, hd, width), BF16),
        pltpu.VMEM((2, batch, hd, width), BF16),
        pltpu.VMEM((2, 2, batch, hd, width), BF16),
        pltpu.VMEM((2, batch, hd, width), F32),
        pltpu.VMEM((2, batch, width), F32),
        pltpu.VMEM((nh, batch, rows, width), BF16),
        pltpu.VMEM((nh, batch, rows, width), BF16),
        pltpu.VMEM((nh, batch, rows, width), F32),
        pltpu.VMEM((nh, batch, rows, width), BF16),
        pltpu.VMEM((nh, bits, batch, rows, width), BF16),
        dma((5,)),
        dma((nh,)),
        dma((nh,)),
        dma((2, nh)),
        dma((2, nh)),
        dma((nh,)),
        dma((nh,)),
        dma((2, 2)),
        dma((2, 2)),
        dma((2, batch)),
        dma((2, batch)),
        dma((2, batch)),
        dma((2, batch)),
        dma((batch, nh)),
        dma((batch, nh)),
        dma((batch, nh)),
        dma((batch, nh)),
    ]
    return pl.pallas_call(
        functools.partial(kernel, n, nh),
        out_shape=jax.ShapeDtypeStruct(tokens.shape, tokens.dtype),
        in_specs=[
            vmem,
            vmem,
            anywhere,
            anywhere,
            vmem,
            vmem,
            vmem,
            vmem,
            anywhere,
            vmem,
            anywhere,
            anywhere,
        ],
        out_specs=vmem,
        scratch_shapes=scratch,
        compiler_params=pltpu.CompilerParams(
            collective_id=0, has_side_effects=True, vmem_limit_bytes=56 * 2**20
        ),
        name="layer",
    )(
        tokens,
        input_norm_gain.reshape(1, -1),
        jnp.transpose(query_key_value_weight, (1, 0, 2)),
        forget_gate_weight,
        jnp.transpose(convolution_filter_taps, (0, 2, 1, 3)),
        slot_forget_rate,
        extra_forget_log,
        head_norm_gain,
        output_projection_weight,
        feedforward_norm_gain.reshape(1, -1),
        up_projection_weight,
        down_projection_weight,
    )


def solution(mesh):
    in_specs = (
        P(None, "seq", "head"),
        P(),
        P(None, None, "head"),
        P(None, "head"),
        P(None, None, None, "head"),
        P("head", None),
        P(None, "seq"),
        P("head", None),
        P("head", None),
        P(),
        P(None, "head"),
        P("head", None),
    )
    out_specs = P(None, "seq", "head")
    return jax.shard_map(
        functools.partial(local, mesh.shape["seq"], mesh.shape["head"]),
        mesh=mesh,
        in_specs=in_specs,
        out_specs=out_specs,
        check_vma=False,
    )
```

```python
import functools

import jax
import jax.numpy as jnp
from jax import lax
from jax.experimental import pallas as pl
from jax.experimental.pallas import tpu as pltpu
from jax.sharding import PartitionSpec as P

SPAN = 64
HALO = 16
PIECES = 4
EPSILON = 1e-06
MESH = pl.DeviceIdType.MESH
F32 = jnp.float32
BF16 = jnp.bfloat16


def mm(a, b, ca=1, cb=0):
    return lax.dot_general(a, b, (((ca,), (cb,)), ((), ())), preferred_element_type=F32)


def split_mm(ones, values, count):
    total, rest = None, values
    for _ in range(count):
        part = rest.astype(BF16)
        rest = rest - part.astype(F32)
        term = mm(ones, part)
        total = term if total is None else total + term
    return total


def mm_split(values, ones, count):
    total, rest = None, values
    for _ in range(count):
        part = rest.astype(BF16)
        rest = rest - part.astype(F32)
        term = mm(part, ones)
        total = term if total is None else total + term
    return total


def one_minus_exp(x):
    series = 1.0 + x * (1 / 2 + x * (1 / 6 + x * (1 / 24 + x * (1 / 120 + x * (1 / 720)))))
    return jnp.where(x > -0.25, -x * series, 1.0 - jnp.exp(x))


def iota(shape, dim):
    return lax.broadcasted_iota(jnp.int32, shape, dim)


class Gather:
    def __init__(self, hx, nh, seq, block, send, recv, direct=False):
        self.hx, self.seq, self.block, self.send, self.recv = hx, seq, block, send, recv
        self.direct = direct
        self.masks = []
        m = nh // 2
        while m:
            self.masks.append(m)
            m //= 2
        self.nh = nh
        self.got = {0}

    def copy(self, o, m):
        ref = self.block(self.hx(o))
        return pltpu.make_async_remote_copy(
            src_ref=ref,
            dst_ref=ref,
            send_sem=self.send.at[o ^ m],
            recv_sem=self.recv.at[o ^ m],
            device_id=(self.seq, self.hx(m)),
            device_id_type=MESH,
        )

    def arrive(self, o):
        if o not in self.got:
            ref = self.block(self.hx(o))
            pltpu.make_async_remote_copy(
                src_ref=ref,
                dst_ref=ref,
                send_sem=self.send.at[o],
                recv_sem=self.recv.at[o],
                device_id=(self.seq, self.hx(1)),
                device_id_type=MESH,
            ).wait_recv()
            self.got.add(o)

    def start(self):
        for m in range(1, self.nh) if self.direct else self.masks:
            self.copy(0, m).start()

    def forward(self):
        if self.direct:
            return
        have = [0]
        for m in self.masks:
            for o in have:
                if o:
                    self.arrive(o)
                    self.copy(o, m).start()
            have = have + [o ^ m for o in have]

    def finish(self):
        for o in range(1, self.nh):
            self.arrive(o)

    def drain(self):
        if self.direct:
            for m in range(1, self.nh):
                self.copy(0, m).wait_send()
            return
        have = [0]
        for m in self.masks:
            for o in have:
                self.copy(o, m).wait_send()
            have = have + [o ^ m for o in have]


def kernel(
    n,
    nh,
    tok,
    gain1,
    wqkv,
    wgate,
    taps,
    rate,
    extra,
    hgain,
    wo,
    gain2,
    wup,
    wdown,
    out,
    xg,
    wq_v,
    wg_v,
    wo_v,
    up_v,
    dn_v,
    nb,
    pj,
    qkv,
    growth_v,
    shrink_v,
    score_v,
    local_v,
    before_v,
    apost,
    arecv,
    fpost,
    frecv,
    cin,
    csend,
    crecv,
    sst,
    begin,
    pair_v,
    pairf_v,
    ag,
    res,
    pf,
    pb,
    rb,
    lsem,
    tok_s,
    tok_r,
    halo_s,
    halo_r,
    wo_s,
    wo_r,
    sib_s,
    sib_r,
    ch_s,
    ch_r,
    st_s,
    st_r,
    at_s,
    at_r,
    rs_s,
    rs_r,
):
    batch, rows, width = tok.shape
    heads, hd = hgain.shape
    spans = rows // SPAN
    s = lax.axis_index("seq")
    h = lax.axis_index("head")

    def hx(o):
        r, bit = h, 1
        while bit <= o:
            if o & bit:
                r = r + bit - 2 * bit * lax.rem(lax.div(r, bit), 2)
            bit *= 2
        return r

    def ring(d):
        return lax.rem(s + d + n, n)

    odd = lax.rem(s, 2)
    pair = lax.div(s, 2)
    pairs = n // 2
    sibling = s + 1 - 2 * odd

    loads = [
        pltpu.make_async_copy(wqkv, wq_v, lsem.at[0]),
        pltpu.make_async_copy(wgate, wg_v, lsem.at[1]),
        pltpu.make_async_copy(wo, wo_v.at[h], lsem.at[2]),
        pltpu.make_async_copy(wup, up_v, lsem.at[3]),
        pltpu.make_async_copy(wdown, dn_v, lsem.at[4]),
    ]
    for load in loads:
        load.start()

    barrier = pltpu.get_barrier_semaphore()
    greeted = [(s, hx(o)) for o in range(1, nh)]
    greeted += [(ring(d), hx(o)) for d in (-1, 1) for o in range(nh)]
    greeted += [(ring(d), h) for d in (-2, 2)]
    for device in greeted:
        pl.semaphore_signal(barrier, inc=1, device_id=device, device_id_type=MESH)
    xg[h, :, HALO : HALO + rows, :] = tok[...]
    cin[...] = jnp.zeros_like(cin)
    pl.semaphore_wait(barrier, len(greeted))

    tokens = Gather(hx, nh, s, lambda i: xg.at[i, :, HALO : HALO + rows, :], tok_s, tok_r)
    tokens.start()
    halos = []
    for o in range(nh):
        for side in (0, 1):
            src = xg.at[h, :, rows : rows + HALO, :] if side == 0 else xg.at[h, :, HALO : 2 * HALO, :]
            at = 0 if side == 0 else HALO + rows
            halos.append(
                pltpu.make_async_remote_copy(
                    src_ref=src,
                    dst_ref=xg.at[h, :, at : at + HALO, :],
                    send_sem=halo_s.at[side, o],
                    recv_sem=halo_r.at[side, o],
                    device_id=(ring(1) if side == 0 else ring(-1), hx(o)),
                    device_id_type=MESH,
                )
            )
    for copy in halos:
        copy.start()
    tokens.forward()
    piece = width // PIECES
    projection = [
        Gather(
            hx, nh, s, lambda i, c=c: wo_v.at[i, c * piece : (c + 1) * piece, :], wo_s.at[c], wo_r.at[c]
        )
        for c in range(PIECES)
    ]
    loads[2].wait()
    projection[0].start()
    projection[1].start()
    tokens.finish()
    for copy in halos:
        copy.wait_recv()

    tall = rows + 2 * HALO
    row_at = iota((tall, 1), 0)
    inside = jnp.logical_and(
        jnp.logical_or(row_at >= HALO, s > 0),
        jnp.logical_or(row_at < HALO + rows, s < n - 1),
    )
    for b in range(batch):
        parts = [xg[j, b].astype(F32) for j in range(nh)]
        square = parts[0] * parts[0]
        for part in parts[1:]:
            square = square + part * part
        mean = jnp.sum(square, axis=1, keepdims=True) / (nh * width)
        scale = jnp.where(inside, lax.rsqrt(mean + EPSILON), 0.0)
        for j in range(nh):
            cols = slice(j * width, (j + 1) * width)
            nb[b, :, cols] = (parts[j] * scale * gain1[:, cols]).astype(BF16)

    loads[0].wait()
    loads[1].wait()
    normed = nb[...].reshape(batch * tall, nh * width)

    def project(i):
        made = mm(normed, wq_v[i]).astype(BF16).astype(F32)
        pj[i] = made.reshape(batch, tall, width)

    def convolve(d, i, b):
        acc = None
        for j in range(4):
            first = HALO + j if d else HALO - j
            term = taps[d, i, j : j + 1, :] * pj[i, b, first : first + rows, :]
            acc = term if acc is None else acc + term
        qkv[d, i, b] = (acc * jax.nn.sigmoid(acc)).astype(BF16)

    project(1)
    project(2)

    lanes = iota((1, width), 1)
    lane_head = lax.div(lanes, hd)
    block_mask = (
        lax.div(iota((width, width), 0), hd) == lax.div(iota((width, width), 1), hd)
    ).astype(F32).astype(BF16)
    causal_t = iota((SPAN, width), 0)
    causal_j = lax.rem(iota((SPAN, width), 1), SPAN)
    causal = [(causal_t >= causal_j).astype(F32), (causal_t <= causal_j).astype(F32)]
    big_t, big_j = iota((rows, rows), 0), iota((rows, rows), 1)
    same = lax.div(big_t, SPAN) == lax.div(big_j, SPAN)
    running = [
        jnp.logical_and(same, big_t >= big_j).astype(F32).astype(BF16),
        jnp.logical_and(same, big_t <= big_j).astype(F32).astype(BF16),
    ]
    rate_row = jnp.concatenate([rate[i : i + 1, :] for i in range(heads)], axis=1)
    gain_row = jnp.concatenate([hgain[i : i + 1, :] for i in range(heads)], axis=1)

    def expand(x):
        return jnp.concatenate([x] * heads, axis=0) * block_mask

    def compact(x):
        total = None
        for i in range(heads):
            term = jnp.where(lane_head == i, x[i * hd : (i + 1) * hd], 0.0)
            total = term if total is None else total + term
        return total

    decays = []
    for b in range(batch):
        logits = mm(nb[b, HALO : HALO + rows, :], wg_v[...])
        column = jnp.sum(
            jnp.where(big_t == big_j, extra[b : b + 1, :], 0.0), axis=1, keepdims=True
        )
        decays.append(-2.0 * rate_row * jax.nn.sigmoid(logits) - column)

    def sib_copies(d):
        return [
            pltpu.make_async_remote_copy(
                src_ref=src,
                dst_ref=dst,
                send_sem=sib_s.at[d, k],
                recv_sem=sib_r.at[d, k],
                device_id=(sibling, h),
                device_id_type=MESH,
            )
            for k, (src, dst) in enumerate(
                ((apost.at[d, 1 - odd], arecv.at[d]), (fpost.at[d], frecv.at[d]))
            )
        ]

    fpost[...] = jnp.zeros_like(fpost)
    order = [list(range(spans)), list(range(spans))[::-1]]
    for d in (0, 1):
        for b in range(batch):
            for i in (1, 2):
                convolve(d, i, b)
            ld = decays[b]
            inflow = one_minus_exp(ld)
            cum = split_mm(running[d], ld, 3)
            growth_v[d, b] = jnp.exp(cum)
            shrink_v[d, b] = (jnp.exp(-cum) * inflow).astype(BF16)
            state = jnp.zeros((2 * hd, width), F32)
            past = jnp.zeros((1, width), F32)
            for g in order[d]:
                r0 = g * SPAN
                local_v[d, b, g] = state
                before_v[d, b, g : g + 1, :] = jnp.exp(past)
                last = r0 if d else r0 + SPAN - 1
                total = cum[last : last + 1, :]
                remain = (jnp.exp(total - cum[r0 : r0 + SPAN]) * inflow[r0 : r0 + SPAN]).astype(BF16)
                new = [
                    compact(mm(qkv[d, i, b, r0 : r0 + SPAN, :], remain, 0, 0)) for i in (1, 2)
                ]
                state = jnp.exp(total) * state + jnp.concatenate(new, axis=0)
                past = past + total
            apost[d, 0, b] = state[:hd].astype(BF16)
            apost[d, 1, b] = state[hd:].astype(BF16)
            fpost[d, b : b + 1, :] = jnp.exp(past)
        for copy in sib_copies(d):
            copy.start()

    project(0)
    for d in (0, 1):
        for b in range(batch):
            convolve(d, 0, b)

    def local_scores(d):
        blocks = [(b, slice(g * SPAN, (g + 1) * SPAN)) for b in range(batch) for g in range(spans)]
        inter = [
            mm(qkv[d, 0, b, span, :], expand(qkv[d, 1, b, span, :]), 1, 1) for b, span in blocks
        ]
        inter = [(x * causal[d]).astype(BF16) for x in inter]
        made = [mm(x, expand(shrink_v[d, b, span, :])) for x, (b, span) in zip(inter, blocks)]
        for x, (b, span) in zip(made, blocks):
            score_v[d, b, span, :] = x

    later = [odd.astype(F32), 1.0 - odd.astype(F32)]
    for d in (0, 1):
        for copy in sib_copies(d):
            copy.wait_recv()
        for b in range(batch):
            mine, other = apost[d, odd, b].astype(F32), arecv[d, b].astype(F32)
            fm, fo = fpost[d, b : b + 1, :], frecv[d, b : b + 1, :]
            pair_v[d, b] = later[d] * (fm * other + mine) + (1.0 - later[d]) * (fo * mine + other)
            pairf_v[d, b : b + 1, :] = fm * fo

    first_pair = [pair == 0, pair == pairs - 1]
    last_pair = [pair == pairs - 1, pair == 0]

    def hop_copy(d, b):
        return pltpu.make_async_remote_copy(
            src_ref=csend.at[d, b],
            dst_ref=crecv.at[d, b],
            send_sem=ch_s.at[d, b],
            recv_sem=ch_r.at[d, b],
            device_id=(ring(-2) if d else ring(2), h),
            device_id_type=MESH,
        )

    def start_copy(d, b):
        return pltpu.make_async_remote_copy(
            src_ref=sst.at[d, b],
            dst_ref=begin.at[d, odd, b],
            send_sem=st_s.at[d, b],
            recv_sem=st_r.at[d, b],
            device_id=(sibling, h),
            device_id_type=MESH,
        )

    def await_start(d, b):
        pltpu.make_async_remote_copy(
            src_ref=sst.at[d, b],
            dst_ref=begin.at[d, 1 - odd, b],
            send_sem=st_s.at[d, b],
            recv_sem=st_r.at[d, b],
            device_id=(sibling, h),
            device_id_type=MESH,
        ).wait_recv()

    def pass_on(d, b):
        csend[d, b] = (pairf_v[d, b : b + 1, :] * cin[d, b] + pair_v[d, b]).astype(BF16)
        hop_copy(d, b).start()

    def open_chain(d):
        @pl.when(jnp.logical_and(first_pair[d], jnp.logical_not(last_pair[d])))
        def _():
            for b in range(batch):
                pass_on(d, b)

    def hop(d):
        for b in range(batch):

            @pl.when(jnp.logical_not(first_pair[d]))
            def _():
                hop_copy(d, b).wait_recv()
                cin[d, b] = crecv[d, b].astype(F32)

            @pl.when(jnp.logical_not(jnp.logical_or(first_pair[d], last_pair[d])))
            def _():
                pass_on(d, b)

            carry = cin[d, b]
            fm, fo = fpost[d, b : b + 1, :], frecv[d, b : b + 1, :]
            mine, other = apost[d, odd, b].astype(F32), arecv[d, b].astype(F32)
            theirs = (1.0 - later[d]) * (fm * carry + mine) + later[d] * carry
            sst[d, b] = theirs.astype(BF16)
            start_copy(d, b).start()
            own = later[d] * (fo * carry + other) + (1.0 - later[d]) * carry
            begin[d, odd, b] = own.astype(BF16)

    lower = 2 * pair < pairs
    open_chain(0)
    open_chain(1)
    projection[2].start()
    local_scores(0)

    @pl.when(lower)
    def _():
        hop(0)

    @pl.when(jnp.logical_not(lower))
    def _():
        hop(1)

    projection[3].start()
    local_scores(1)

    @pl.when(lower)
    def _():
        hop(1)

    @pl.when(jnp.logical_not(lower))
    def _():
        hop(0)

    for member in projection[:2]:
        member.forward()

    attends = [
        Gather(hx, nh, s, lambda i, b=b: ag.at[i, b], at_s.at[b], at_r.at[b], b + 1 < batch)
        for b in range(batch)
    ]
    group = min(width, 128)

    def head_max(x):
        tops = []
        for c in range(0, width, group):
            part, head = x[:, c : c + group], lane_head[:, c : c + group]
            top = None
            for i in range(c // hd, (c + group) // hd):
                best = jnp.max(jnp.where(head == i, part, -jnp.inf), axis=1, keepdims=True)
                top = best if top is None else jnp.where(head == i, best, top)
            tops.append(jnp.broadcast_to(top, part.shape))
        return jnp.concatenate(tops, axis=1)

    for b in range(batch):
        for d in (0, 1):
            await_start(d, b)
        blocks = [(d, g, slice(g * SPAN, (g + 1) * SPAN)) for g in range(spans) for d in (0, 1)]
        keys, values = [
            [
                (
                    before_v[d, b, g : g + 1, :] * begin[d, i, b].astype(F32)
                    + local_v[d, b, g, i * hd : (i + 1) * hd, :]
                ).astype(BF16)
                for d, g, span in blocks
            ]
            for i in (0, 1)
        ]
        growth = [growth_v[d, b, span, :] for d, g, span in blocks]
        scores = [mm(qkv[d, 0, b, span, :], expand(k)) for (d, g, span), k in zip(blocks, keys)]
        scores = [
            w * (score_v[d, b, span, :] + x) for (d, g, span), x, w in zip(blocks, scores, growth)
        ]
        power = [jnp.exp(x - head_max(x)) for x in scores]
        norm = [mm(x.astype(BF16), block_mask) for x in power]
        weighted = [(x / y * w).astype(BF16) for x, y, w in zip(power, norm, growth)]
        mixing = [
            mm(x, expand(shrink_v[d, b, span, :]), 1, 1) for (d, g, span), x in zip(blocks, weighted)
        ]
        mixing = [(x * causal[d]).astype(BF16) for (d, g, span), x in zip(blocks, mixing)]
        carried = [mm(x, expand(v), 1, 1) for x, v in zip(weighted, values)]
        made = [
            x + mm(y, expand(qkv[d, 2, b, span, :]))
            for (d, g, span), x, y in zip(blocks, carried, mixing)
        ]
        mean = [mm((x * x).astype(BF16), block_mask) / hd for x in made]
        made = [x * lax.rsqrt(y + EPSILON) * gain_row for x, y in zip(made, mean)]
        for g in range(spans):
            span = slice(g * SPAN, (g + 1) * SPAN)
            ag[h, b, span, :] = (made[2 * g] + made[2 * g + 1]).astype(BF16)
        attends[b].start()
        if b == 0:
            for member in projection[2:]:
                member.forward()
    attends[0].forward()

    for member in projection:
        member.finish()
    loads[3].wait()
    loads[4].wait()

    masks = [1 << i for i in range(nh.bit_length() - 1)]

    def rs_copy(b, o, m):
        return pltpu.make_async_remote_copy(
            src_ref=pb.at[hx(o), b],
            dst_ref=rb.at[o ^ m, m.bit_length() - 1, b],
            send_sem=rs_s.at[b, o],
            recv_sem=rs_r.at[b, o],
            device_id=(s, hx(m)),
            device_id_type=MESH,
        )

    leaving = sorted(range(nh), key=lambda o: [-((o >> k) & 1) for k in range(len(masks))])

    def level(o):
        return next((k for k, m in enumerate(masks) if o & m), len(masks))

    def settle(b, o):
        total = pf[hx(o), b]
        for k in range(level(o)):
            rs_copy(b, o ^ masks[k], masks[k]).wait_recv()
            total = total + rb[o, k, b].astype(F32)
        if o:
            pb[hx(o), b] = total.astype(BF16)
            rs_copy(b, o, masks[level(o)]).start()
        else:
            out[b] = (res[h, b].astype(F32) + total).astype(BF16)

    wo_all = wo_v[...].reshape(nh * width, nh * width)
    for b in range(batch):
        attends[b].finish()
        attention = jnp.concatenate([ag[j, b] for j in range(nh)], axis=1)
        whole = jnp.concatenate([xg[j, b, HALO : HALO + rows, :] for j in range(nh)], axis=1)
        residual = (whole.astype(F32) + mm(attention, wo_all)).astype(BF16)
        wide = residual.astype(F32)
        for j in range(nh):
            res[j, b] = residual[:, j * width : (j + 1) * width]
        mean = jnp.mean(wide * wide, axis=1, keepdims=True)
        mlp_in = (wide * lax.rsqrt(mean + EPSILON) * gain2[...]).astype(BF16)
        hidden = jax.nn.gelu(mm(mlp_in, up_v[...])).astype(BF16)
        if b + 1 < batch:
            attends[b + 1].forward()
        if b:
            for o in leaving:
                if 0 < level(o) < len(masks):
                    settle(b - 1, o)
        for o in leaving:
            cols = pl.ds(pl.multiple_of(hx(o) * width, width), width)
            made = mm(hidden, dn_v[:, cols])
            if level(o) == 0 and o:
                pb[hx(o), b] = made.astype(BF16)
                rs_copy(b, o, masks[0]).start()
            else:
                pf[hx(o), b] = made
                if o and b == batch - 1:
                    settle(b, o)
    for b in range(batch):
        settle(b, 0)

    tokens.drain()
    for member in projection:
        member.drain()
    for copy in halos:
        copy.wait_send()
    for d in (0, 1):
        for copy in sib_copies(d):
            copy.wait_send()

        @pl.when(jnp.logical_not(last_pair[d]))
        def _():
            for b in range(batch):
                hop_copy(d, b).wait_send()

        for b in range(batch):
            start_copy(d, b).wait_send()

    for b in range(batch):
        attends[b].drain()
        for o in range(1, nh):
            rs_copy(b, o, masks[level(o)]).wait_send()


def local(
    n,
    nh,
    tokens,
    input_norm_gain,
    query_key_value_weight,
    forget_gate_weight,
    convolution_filter_taps,
    slot_forget_rate,
    extra_forget_log,
    head_norm_gain,
    output_projection_weight,
    feedforward_norm_gain,
    up_projection_weight,
    down_projection_weight,
):
    batch, rows, width = tokens.shape
    depth = nh * width
    hidden = up_projection_weight.shape[1]
    spans = rows // SPAN
    hd = head_norm_gain.shape[1]
    tall = rows + 2 * HALO
    vmem = pl.BlockSpec(memory_space=pltpu.VMEM)
    anywhere = pl.BlockSpec(memory_space=pl.ANY)
    dma = pltpu.SemaphoreType.DMA
    bits = nh.bit_length() - 1
    scratch = [
        pltpu.VMEM((nh, batch, tall, width), BF16),
        pltpu.VMEM((3, depth, width), BF16),
        pltpu.VMEM((depth, width), BF16),
        pltpu.VMEM((nh, width, depth), BF16),
        pltpu.VMEM((depth, hidden), BF16),
        pltpu.VMEM((hidden, depth), BF16),
        pltpu.VMEM((batch, tall, depth), BF16),
        pltpu.VMEM((3, batch, tall, width), F32),
        pltpu.VMEM((2, 3, batch, rows, width), BF16),
        pltpu.VMEM((2, batch, rows, width), F32),
        pltpu.VMEM((2, batch, rows, width), BF16),
        pltpu.VMEM((2, batch, rows, width), F32),
        pltpu.VMEM((2, batch, spans, 2 * hd, width), F32),
        pltpu.VMEM((2, batch, spans, width), F32),
        pltpu.VMEM((2, 2, batch, hd, width), BF16),
        pltpu.VMEM((2, batch, hd, width), BF16),
        pltpu.VMEM((2, 8 * pl.cdiv(batch, 8), width), F32),
        pltpu.VMEM((2, 8 * pl.cdiv(batch, 8), width), F32),
        pltpu.VMEM((2, batch, hd, width), F32),
        pltpu.VMEM((2, batch, hd, width), BF16),
        pltpu.VMEM((2, batch, hd, width), BF16),
        pltpu.VMEM((2, batch, hd, width), BF16),
        pltpu.VMEM((2, 2, batch, hd, width), BF16),
        pltpu.VMEM((2, batch, hd, width), F32),
        pltpu.VMEM((2, batch, width), F32),
        pltpu.VMEM((nh, batch, rows, width), BF16),
        pltpu.VMEM((nh, batch, rows, width), BF16),
        pltpu.VMEM((nh, batch, rows, width), F32),
        pltpu.VMEM((nh, batch, rows, width), BF16),
        pltpu.VMEM((nh, bits, batch, rows, width), BF16),
        dma((5,)),
        dma((nh,)),
        dma((nh,)),
        dma((2, nh)),
        dma((2, nh)),
        dma((PIECES, nh)),
        dma((PIECES, nh)),
        dma((2, 2)),
        dma((2, 2)),
        dma((2, batch)),
        dma((2, batch)),
        dma((2, batch)),
        dma((2, batch)),
        dma((batch, nh)),
        dma((batch, nh)),
        dma((batch, nh)),
        dma((batch, nh)),
    ]
    return pl.pallas_call(
        functools.partial(kernel, n, nh),
        out_shape=jax.ShapeDtypeStruct(tokens.shape, tokens.dtype),
        in_specs=[
            vmem,
            vmem,
            anywhere,
            anywhere,
            vmem,
            vmem,
            vmem,
            vmem,
            anywhere,
            vmem,
            anywhere,
            anywhere,
        ],
        out_specs=vmem,
        scratch_shapes=scratch,
        compiler_params=pltpu.CompilerParams(
            collective_id=0, has_side_effects=True, vmem_limit_bytes=56 * 2**20
        ),
        name="layer",
    )(
        tokens,
        input_norm_gain.reshape(1, -1),
        jnp.transpose(query_key_value_weight, (1, 0, 2)),
        forget_gate_weight,
        jnp.transpose(convolution_filter_taps, (0, 2, 1, 3)),
        slot_forget_rate,
        extra_forget_log,
        head_norm_gain,
        output_projection_weight,
        feedforward_norm_gain.reshape(1, -1),
        up_projection_weight,
        down_projection_weight,
    )


def solution(mesh):
    in_specs = (
        P(None, "seq", "head"),
        P(),
        P(None, None, "head"),
        P(None, "head"),
        P(None, None, None, "head"),
        P("head", None),
        P(None, "seq"),
        P("head", None),
        P("head", None),
        P(),
        P(None, "head"),
        P("head", None),
    )
    out_specs = P(None, "seq", "head")
    return jax.shard_map(
        functools.partial(local, mesh.shape["seq"], mesh.shape["head"]),
        mesh=mesh,
        in_specs=in_specs,
        out_specs=out_specs,
        check_vma=False,
    )
```

```python
import functools

import jax
import jax.numpy as jnp
from jax import lax
from jax.experimental import pallas as pl
from jax.experimental.pallas import tpu as pltpu
from jax.sharding import PartitionSpec as P

SPAN = 64
HALO = 16
PIECES = 4
EPSILON = 1e-06
MESH = pl.DeviceIdType.MESH
F32 = jnp.float32
BF16 = jnp.bfloat16


def mm(a, b, ca=1, cb=0):
    return lax.dot_general(a, b, (((ca,), (cb,)), ((), ())), preferred_element_type=F32)


def split_mm(ones, values, count):
    total, rest = None, values
    for _ in range(count):
        part = rest.astype(BF16)
        rest = rest - part.astype(F32)
        term = mm(ones, part)
        total = term if total is None else total + term
    return total


def mm_split(values, ones, count):
    total, rest = None, values
    for _ in range(count):
        part = rest.astype(BF16)
        rest = rest - part.astype(F32)
        term = mm(part, ones)
        total = term if total is None else total + term
    return total


def one_minus_exp(x):
    series = 1.0 + x * (1 / 2 + x * (1 / 6 + x * (1 / 24 + x * (1 / 120 + x * (1 / 720)))))
    return jnp.where(x > -0.25, -x * series, 1.0 - jnp.exp(x))


def iota(shape, dim):
    return lax.broadcasted_iota(jnp.int32, shape, dim)


class Gather:
    def __init__(self, hx, nh, seq, block, send, recv, direct=False):
        self.hx, self.seq, self.block, self.send, self.recv = hx, seq, block, send, recv
        self.direct = direct
        self.masks = []
        m = nh // 2
        while m:
            self.masks.append(m)
            m //= 2
        self.nh = nh
        self.got = {0}

    def copy(self, o, m):
        ref = self.block(self.hx(o))
        return pltpu.make_async_remote_copy(
            src_ref=ref,
            dst_ref=ref,
            send_sem=self.send.at[o ^ m],
            recv_sem=self.recv.at[o ^ m],
            device_id=(self.seq, self.hx(m)),
            device_id_type=MESH,
        )

    def arrive(self, o):
        if o not in self.got:
            ref = self.block(self.hx(o))
            pltpu.make_async_remote_copy(
                src_ref=ref,
                dst_ref=ref,
                send_sem=self.send.at[o],
                recv_sem=self.recv.at[o],
                device_id=(self.seq, self.hx(1)),
                device_id_type=MESH,
            ).wait_recv()
            self.got.add(o)

    def start(self):
        for m in range(1, self.nh) if self.direct else self.masks:
            self.copy(0, m).start()

    def forward(self):
        if self.direct:
            return
        have = [0]
        for m in self.masks:
            for o in have:
                if o:
                    self.arrive(o)
                    self.copy(o, m).start()
            have = have + [o ^ m for o in have]

    def finish(self):
        for o in range(1, self.nh):
            self.arrive(o)

    def drain(self):
        if self.direct:
            for m in range(1, self.nh):
                self.copy(0, m).wait_send()
            return
        have = [0]
        for m in self.masks:
            for o in have:
                self.copy(o, m).wait_send()
            have = have + [o ^ m for o in have]


def kernel(
    n,
    nh,
    tok,
    gain1,
    wqkv,
    wgate,
    taps,
    rate,
    extra,
    hgain,
    wo,
    gain2,
    wup,
    wdown,
    out,
    xg,
    wq_v,
    wg_v,
    wo_v,
    up_v,
    dn_v,
    nb,
    pj,
    qkv,
    growth_v,
    shrink_v,
    score_v,
    local_v,
    before_v,
    apost,
    arecv,
    fpost,
    frecv,
    cin,
    csend,
    crecv,
    sst,
    begin,
    pair_v,
    pairf_v,
    ag,
    res,
    pf,
    pb,
    rb,
    lsem,
    tok_s,
    tok_r,
    halo_s,
    halo_r,
    wo_s,
    wo_r,
    sib_s,
    sib_r,
    ch_s,
    ch_r,
    st_s,
    st_r,
    at_s,
    at_r,
    rs_s,
    rs_r,
):
    batch, rows, width = tok.shape
    heads, hd = hgain.shape
    spans = rows // SPAN
    s = lax.axis_index("seq")
    h = lax.axis_index("head")

    def hx(o):
        r, bit = h, 1
        while bit <= o:
            if o & bit:
                r = r + bit - 2 * bit * lax.rem(lax.div(r, bit), 2)
            bit *= 2
        return r

    def ring(d):
        return lax.rem(s + d + n, n)

    odd = lax.rem(s, 2)
    pair = lax.div(s, 2)
    pairs = n // 2
    sibling = s + 1 - 2 * odd

    loads = [
        pltpu.make_async_copy(wqkv, wq_v, lsem.at[0]),
        pltpu.make_async_copy(wgate, wg_v, lsem.at[1]),
        pltpu.make_async_copy(wo, wo_v.at[h], lsem.at[2]),
        pltpu.make_async_copy(wup, up_v, lsem.at[3]),
        pltpu.make_async_copy(wdown, dn_v, lsem.at[4]),
    ]
    for load in loads:
        load.start()

    barrier = pltpu.get_barrier_semaphore()
    greeted = [(s, hx(o)) for o in range(1, nh)]
    greeted += [(ring(d), hx(o)) for d in (-1, 1) for o in range(nh)]
    greeted += [(ring(d), h) for d in (-2, 2)]
    for device in greeted:
        pl.semaphore_signal(barrier, inc=1, device_id=device, device_id_type=MESH)
    xg[h, :, HALO : HALO + rows, :] = tok[...]
    cin[...] = jnp.zeros_like(cin)
    pl.semaphore_wait(barrier, len(greeted))

    tokens = [
        Gather(
            hx, nh, s, lambda i, b=b: xg.at[i, b, HALO : HALO + rows, :], tok_s.at[b], tok_r.at[b]
        )
        for b in range(batch)
    ]
    tokens[0].start()
    halos = []
    for o in range(nh):
        for side in (0, 1):
            src = xg.at[h, :, rows : rows + HALO, :] if side == 0 else xg.at[h, :, HALO : 2 * HALO, :]
            at = 0 if side == 0 else HALO + rows
            halos.append(
                pltpu.make_async_remote_copy(
                    src_ref=src,
                    dst_ref=xg.at[h, :, at : at + HALO, :],
                    send_sem=halo_s.at[side, o],
                    recv_sem=halo_r.at[side, o],
                    device_id=(ring(1) if side == 0 else ring(-1), hx(o)),
                    device_id_type=MESH,
                )
            )
    for copy in halos:
        copy.start()
    for b in range(1, batch):
        tokens[b].start()
    tokens[0].forward()
    piece = width // PIECES
    projection = [
        Gather(
            hx, nh, s, lambda i, c=c: wo_v.at[i, c * piece : (c + 1) * piece, :], wo_s.at[c], wo_r.at[c]
        )
        for c in range(PIECES)
    ]
    tokens[0].finish()
    for copy in halos:
        copy.wait_recv()
    loads[2].wait()

    tall = rows + 2 * HALO
    row_at = iota((tall, 1), 0)
    inside = jnp.logical_and(
        jnp.logical_or(row_at >= HALO, s > 0),
        jnp.logical_or(row_at < HALO + rows, s < n - 1),
    )
    def norm_in(b):
        parts = [xg[j, b].astype(F32) for j in range(nh)]
        square = parts[0] * parts[0]
        for part in parts[1:]:
            square = square + part * part
        mean = jnp.sum(square, axis=1, keepdims=True) / (nh * width)
        scale = jnp.where(inside, lax.rsqrt(mean + EPSILON), 0.0)
        for j in range(nh):
            cols = slice(j * width, (j + 1) * width)
            nb[b, :, cols] = (parts[j] * scale * gain1[:, cols]).astype(BF16)

    def project(i, b):
        pj[i, b] = mm(nb[b], wq_v[i]).astype(BF16).astype(F32)

    def convolve(d, i, b):
        acc = None
        for j in range(4):
            first = HALO + j if d else HALO - j
            term = taps[d, i, j : j + 1, :] * pj[i, b, first : first + rows, :]
            acc = term if acc is None else acc + term
        qkv[d, i, b] = (acc * jax.nn.sigmoid(acc)).astype(BF16)

    lanes = iota((1, width), 1)
    lane_head = lax.div(lanes, hd)
    block_mask = (
        lax.div(iota((width, width), 0), hd) == lax.div(iota((width, width), 1), hd)
    ).astype(F32).astype(BF16)
    causal_t = iota((SPAN, width), 0)
    causal_j = lax.rem(iota((SPAN, width), 1), SPAN)
    causal = [(causal_t >= causal_j).astype(F32), (causal_t <= causal_j).astype(F32)]
    big_t, big_j = iota((rows, rows), 0), iota((rows, rows), 1)
    same = lax.div(big_t, SPAN) == lax.div(big_j, SPAN)
    running = [
        jnp.logical_and(same, big_t >= big_j).astype(F32).astype(BF16),
        jnp.logical_and(same, big_t <= big_j).astype(F32).astype(BF16),
    ]
    rate_row = jnp.concatenate([rate[i : i + 1, :] for i in range(heads)], axis=1)
    gain_row = jnp.concatenate([hgain[i : i + 1, :] for i in range(heads)], axis=1)

    def expand(x):
        return jnp.concatenate([x] * heads, axis=0) * block_mask

    def compact(x):
        total = None
        for i in range(heads):
            term = jnp.where(lane_head == i, x[i * hd : (i + 1) * hd], 0.0)
            total = term if total is None else total + term
        return total

    def decay(b):
        logits = mm(nb[b, HALO : HALO + rows, :], wg_v[...])
        column = jnp.sum(
            jnp.where(big_t == big_j, extra[b : b + 1, :], 0.0), axis=1, keepdims=True
        )
        return -2.0 * rate_row * jax.nn.sigmoid(logits) - column

    def sib_copies(d, b):
        return [
            pltpu.make_async_remote_copy(
                src_ref=src,
                dst_ref=dst,
                send_sem=sib_s.at[d, b, k],
                recv_sem=sib_r.at[d, b, k],
                device_id=(sibling, h),
                device_id_type=MESH,
            )
            for k, (src, dst) in enumerate(
                ((apost.at[d, 1 - odd, b], arecv.at[d, b]), (fpost.at[d, b], frecv.at[d, b]))
            )
        ]

    order = [list(range(spans)), list(range(spans))[::-1]]

    def summarize(b):
        ld = decay(b)
        inflow = one_minus_exp(ld)
        for d in (0, 1):
            for i in (1, 2):
                convolve(d, i, b)
            cum = split_mm(running[d], ld, 3)
            growth_v[d, b] = jnp.exp(cum)
            shrink_v[d, b] = (jnp.exp(-cum) * inflow).astype(BF16)
            state = jnp.zeros((2 * hd, width), F32)
            past = jnp.zeros((1, width), F32)
            for g in order[d]:
                r0 = g * SPAN
                local_v[d, b, g] = state
                before_v[d, b, g : g + 1, :] = jnp.exp(past)
                last = r0 if d else r0 + SPAN - 1
                total = cum[last : last + 1, :]
                remain = (jnp.exp(total - cum[r0 : r0 + SPAN]) * inflow[r0 : r0 + SPAN]).astype(BF16)
                new = [
                    compact(mm(qkv[d, i, b, r0 : r0 + SPAN, :], remain, 0, 0)) for i in (1, 2)
                ]
                state = jnp.exp(total) * state + jnp.concatenate(new, axis=0)
                past = past + total
            apost[d, 0, b] = state[:hd].astype(BF16)
            apost[d, 1, b] = state[hd:].astype(BF16)
            fpost[d, b] = jnp.broadcast_to(jnp.exp(past), (8, width))
            for copy in sib_copies(d, b):
                copy.start()

    def local_scores(b):
        project(0, b)
        for d in (0, 1):
            convolve(d, 0, b)
        blocks = [(d, slice(g * SPAN, (g + 1) * SPAN)) for g in range(spans) for d in (0, 1)]
        inter = [
            mm(qkv[d, 0, b, span, :], expand(qkv[d, 1, b, span, :]), 1, 1) for d, span in blocks
        ]
        inter = [(x * causal[d]).astype(BF16) for x, (d, span) in zip(inter, blocks)]
        made = [mm(x, expand(shrink_v[d, b, span, :])) for x, (d, span) in zip(inter, blocks)]
        for x, (d, span) in zip(made, blocks):
            score_v[d, b, span, :] = x

    later = [odd.astype(F32), 1.0 - odd.astype(F32)]

    def join(b):
        for d in (0, 1):
            for copy in sib_copies(d, b):
                copy.wait_recv()
            mine, other = apost[d, odd, b].astype(F32), arecv[d, b].astype(F32)
            fm, fo = fpost[d, b, :1, :], frecv[d, b, :1, :]
            pair_v[d, b] = later[d] * (fm * other + mine) + (1.0 - later[d]) * (fo * mine + other)
            pairf_v[d, b] = jnp.broadcast_to(fm * fo, (8, width))
            open_chain(d, b)

    first_pair = [pair == 0, pair == pairs - 1]
    last_pair = [pair == pairs - 1, pair == 0]

    def hop_copy(d, b):
        return pltpu.make_async_remote_copy(
            src_ref=csend.at[d, b],
            dst_ref=crecv.at[d, b],
            send_sem=ch_s.at[d, b],
            recv_sem=ch_r.at[d, b],
            device_id=(ring(-2) if d else ring(2), h),
            device_id_type=MESH,
        )

    def start_copy(d, b):
        return pltpu.make_async_remote_copy(
            src_ref=sst.at[d, b],
            dst_ref=begin.at[d, odd, b],
            send_sem=st_s.at[d, b],
            recv_sem=st_r.at[d, b],
            device_id=(sibling, h),
            device_id_type=MESH,
        )

    def await_start(d, b):
        pltpu.make_async_remote_copy(
            src_ref=sst.at[d, b],
            dst_ref=begin.at[d, 1 - odd, b],
            send_sem=st_s.at[d, b],
            recv_sem=st_r.at[d, b],
            device_id=(sibling, h),
            device_id_type=MESH,
        ).wait_recv()

    def pass_on(d, b):
        csend[d, b] = (pairf_v[d, b, :1, :] * cin[d, b] + pair_v[d, b]).astype(BF16)
        hop_copy(d, b).start()

    def open_chain(d, b):
        @pl.when(jnp.logical_and(first_pair[d], jnp.logical_not(last_pair[d])))
        def _():
            pass_on(d, b)

    def hop(d, b):
        @pl.when(jnp.logical_not(first_pair[d]))
        def _():
            hop_copy(d, b).wait_recv()
            cin[d, b] = crecv[d, b].astype(F32)

        @pl.when(jnp.logical_not(jnp.logical_or(first_pair[d], last_pair[d])))
        def _():
            pass_on(d, b)

        carry = cin[d, b]
        fm, fo = fpost[d, b, :1, :], frecv[d, b, :1, :]
        mine, other = apost[d, odd, b].astype(F32), arecv[d, b].astype(F32)
        theirs = (1.0 - later[d]) * (fm * carry + mine) + later[d] * carry
        sst[d, b] = theirs.astype(BF16)
        start_copy(d, b).start()
        own = later[d] * (fo * carry + other) + (1.0 - later[d]) * carry
        begin[d, odd, b] = own.astype(BF16)

    lower = 2 * pair < pairs
    upper = jnp.logical_not(lower)

    def near(b):
        pl.when(lower)(lambda: hop(0, b))
        pl.when(upper)(lambda: hop(1, b))

    def far(b, ends):
        for d, side in ((1, lower), (0, upper)):
            end = last_pair[d] if ends else jnp.logical_not(last_pair[d])
            pl.when(jnp.logical_and(side, end))(functools.partial(hop, d, b))

    norm_in(0)
    loads[0].wait()
    loads[1].wait()
    project(1, 0)
    project(2, 0)
    for b in range(1, batch):
        tokens[b].forward()
    projection[0].start()
    summarize(0)
    for b in range(1, batch):
        tokens[b].finish()
        norm_in(b)
        project(1, b)
        project(2, b)
        join(b - 1)
        projection[1].start() if b == 1 else None
        summarize(b)
    if batch == 1:
        projection[1].start()
    for b in range(batch):
        if b:
            near(b - 1)
        if b == batch - 1:
            join(b)
        local_scores(b)
        if b:
            far(b - 1, False)
            far(b - 1, True)
        projection[2 + b].start() if b < 2 else None
    near(batch - 1)
    far(batch - 1, False)
    if batch == 1:
        projection[3].start()
    for member in projection[:1]:
        member.forward()

    attends = [
        Gather(hx, nh, s, lambda i, b=b: ag.at[i, b], at_s.at[b], at_r.at[b], b + 1 < batch)
        for b in range(batch)
    ]
    group = min(width, 128)

    def head_max(x):
        tops = []
        for c in range(0, width, group):
            part, head = x[:, c : c + group], lane_head[:, c : c + group]
            top = None
            for i in range(c // hd, (c + group) // hd):
                best = jnp.max(jnp.where(head == i, part, -jnp.inf), axis=1, keepdims=True)
                top = best if top is None else jnp.where(head == i, best, top)
            tops.append(jnp.broadcast_to(top, part.shape))
        return jnp.concatenate(tops, axis=1)

    def stacked(xs):
        sums = mm(jnp.concatenate([x.astype(BF16) for x in xs], axis=0), block_mask)
        return [sums[i * SPAN : (i + 1) * SPAN] for i in range(len(xs))]

    for b in range(batch):
        if b == batch - 1:
            far(b, True)
        for d in (0, 1):
            await_start(d, b)
        blocks = [(d, g, slice(g * SPAN, (g + 1) * SPAN)) for g in range(spans) for d in (0, 1)]
        keys, values = [
            [
                (
                    before_v[d, b, g : g + 1, :] * begin[d, i, b].astype(F32)
                    + local_v[d, b, g, i * hd : (i + 1) * hd, :]
                ).astype(BF16)
                for d, g, span in blocks
            ]
            for i in (0, 1)
        ]
        growth = [growth_v[d, b, span, :] for d, g, span in blocks]
        scores = [mm(qkv[d, 0, b, span, :], expand(k)) for (d, g, span), k in zip(blocks, keys)]
        scores = [
            w * (score_v[d, b, span, :] + x) for (d, g, span), x, w in zip(blocks, scores, growth)
        ]
        power = [jnp.exp(x - head_max(x)) for x in scores]
        norm = stacked(power)
        weighted = [(x / y * w).astype(BF16) for x, y, w in zip(power, norm, growth)]
        mixing = [
            mm(x, expand(shrink_v[d, b, span, :]), 1, 1) for (d, g, span), x in zip(blocks, weighted)
        ]
        mixing = [(x * causal[d]).astype(BF16) for (d, g, span), x in zip(blocks, mixing)]
        carried = [mm(x, expand(v), 1, 1) for x, v in zip(weighted, values)]
        made = [
            x + mm(y, expand(qkv[d, 2, b, span, :]))
            for (d, g, span), x, y in zip(blocks, carried, mixing)
        ]
        mean = [x / hd for x in stacked([x * x for x in made])]
        made = [x * lax.rsqrt(y + EPSILON) * gain_row for x, y in zip(made, mean)]
        for g in range(spans):
            span = slice(g * SPAN, (g + 1) * SPAN)
            ag[h, b, span, :] = (made[2 * g] + made[2 * g + 1]).astype(BF16)
        attends[b].start()
        if b == 0:
            for member in projection[1:]:
                member.forward()
    attends[0].forward()

    for member in projection:
        member.finish()
    loads[3].wait()
    loads[4].wait()

    masks = [1 << i for i in range(nh.bit_length() - 1)]

    def rs_copy(b, o, m):
        return pltpu.make_async_remote_copy(
            src_ref=pb.at[hx(o), b],
            dst_ref=rb.at[o ^ m, m.bit_length() - 1, b],
            send_sem=rs_s.at[b, o],
            recv_sem=rs_r.at[b, o],
            device_id=(s, hx(m)),
            device_id_type=MESH,
        )

    leaving = sorted(range(nh), key=lambda o: [-((o >> k) & 1) for k in range(len(masks))])

    def level(o):
        return next((k for k, m in enumerate(masks) if o & m), len(masks))

    def settle(b, o):
        total = pf[hx(o), b]
        for k in range(level(o)):
            rs_copy(b, o ^ masks[k], masks[k]).wait_recv()
            total = total + rb[o, k, b].astype(F32)
        if o:
            pb[hx(o), b] = total.astype(BF16)
            rs_copy(b, o, masks[level(o)]).start()
        else:
            out[b] = (res[h, b].astype(F32) + total).astype(BF16)

    wo_all = wo_v[...].reshape(nh * width, nh * width)
    for b in range(batch):
        attends[b].finish()
        attention = jnp.concatenate([ag[j, b] for j in range(nh)], axis=1)
        whole = jnp.concatenate([xg[j, b, HALO : HALO + rows, :] for j in range(nh)], axis=1)
        residual = (whole.astype(F32) + mm(attention, wo_all)).astype(BF16)
        wide = residual.astype(F32)
        for j in range(nh):
            res[j, b] = residual[:, j * width : (j + 1) * width]
        mean = jnp.mean(wide * wide, axis=1, keepdims=True)
        mlp_in = (wide * lax.rsqrt(mean + EPSILON) * gain2[...]).astype(BF16)
        hidden = jax.nn.gelu(mm(mlp_in, up_v[...])).astype(BF16)
        if b + 1 < batch:
            attends[b + 1].forward()
        if b:
            for o in leaving:
                if 0 < level(o) < len(masks):
                    settle(b - 1, o)
        for o in leaving:
            cols = pl.ds(pl.multiple_of(hx(o) * width, width), width)
            made = mm(hidden, dn_v[:, cols])
            if level(o) == 0 and o:
                pb[hx(o), b] = made.astype(BF16)
                rs_copy(b, o, masks[0]).start()
            else:
                pf[hx(o), b] = made
                if o and b == batch - 1:
                    settle(b, o)
    for b in range(batch):
        settle(b, 0)

    for member in tokens:
        member.drain()
    for member in projection:
        member.drain()
    for copy in halos:
        copy.wait_send()
    for d in (0, 1):
        for b in range(batch):
            for copy in sib_copies(d, b):
                copy.wait_send()

        @pl.when(jnp.logical_not(last_pair[d]))
        def _():
            for b in range(batch):
                hop_copy(d, b).wait_send()

        for b in range(batch):
            start_copy(d, b).wait_send()

    for b in range(batch):
        attends[b].drain()
        for o in range(1, nh):
            rs_copy(b, o, masks[level(o)]).wait_send()


def local(
    n,
    nh,
    tokens,
    input_norm_gain,
    query_key_value_weight,
    forget_gate_weight,
    convolution_filter_taps,
    slot_forget_rate,
    extra_forget_log,
    head_norm_gain,
    output_projection_weight,
    feedforward_norm_gain,
    up_projection_weight,
    down_projection_weight,
):
    batch, rows, width = tokens.shape
    depth = nh * width
    hidden = up_projection_weight.shape[1]
    spans = rows // SPAN
    hd = head_norm_gain.shape[1]
    tall = rows + 2 * HALO
    vmem = pl.BlockSpec(memory_space=pltpu.VMEM)
    anywhere = pl.BlockSpec(memory_space=pl.ANY)
    dma = pltpu.SemaphoreType.DMA
    bits = nh.bit_length() - 1
    scratch = [
        pltpu.VMEM((nh, batch, tall, width), BF16),
        pltpu.VMEM((3, depth, width), BF16),
        pltpu.VMEM((depth, width), BF16),
        pltpu.VMEM((nh, width, depth), BF16),
        pltpu.VMEM((depth, hidden), BF16),
        pltpu.VMEM((hidden, depth), BF16),
        pltpu.VMEM((batch, tall, depth), BF16),
        pltpu.VMEM((3, batch, tall, width), F32),
        pltpu.VMEM((2, 3, batch, rows, width), BF16),
        pltpu.VMEM((2, batch, rows, width), F32),
        pltpu.VMEM((2, batch, rows, width), BF16),
        pltpu.VMEM((2, batch, rows, width), F32),
        pltpu.VMEM((2, batch, spans, 2 * hd, width), F32),
        pltpu.VMEM((2, batch, spans, width), F32),
        pltpu.VMEM((2, 2, batch, hd, width), BF16),
        pltpu.VMEM((2, batch, hd, width), BF16),
        pltpu.VMEM((2, batch, 8, width), F32),
        pltpu.VMEM((2, batch, 8, width), F32),
        pltpu.VMEM((2, batch, hd, width), F32),
        pltpu.VMEM((2, batch, hd, width), BF16),
        pltpu.VMEM((2, batch, hd, width), BF16),
        pltpu.VMEM((2, batch, hd, width), BF16),
        pltpu.VMEM((2, 2, batch, hd, width), BF16),
        pltpu.VMEM((2, batch, hd, width), F32),
        pltpu.VMEM((2, batch, 8, width), F32),
        pltpu.VMEM((nh, batch, rows, width), BF16),
        pltpu.VMEM((nh, batch, rows, width), BF16),
        pltpu.VMEM((nh, batch, rows, width), F32),
        pltpu.VMEM((nh, batch, rows, width), BF16),
        pltpu.VMEM((nh, bits, batch, rows, width), BF16),
        dma((5,)),
        dma((batch, nh)),
        dma((batch, nh)),
        dma((2, nh)),
        dma((2, nh)),
        dma((PIECES, nh)),
        dma((PIECES, nh)),
        dma((2, batch, 2)),
        dma((2, batch, 2)),
        dma((2, batch)),
        dma((2, batch)),
        dma((2, batch)),
        dma((2, batch)),
        dma((batch, nh)),
        dma((batch, nh)),
        dma((batch, nh)),
        dma((batch, nh)),
    ]
    return pl.pallas_call(
        functools.partial(kernel, n, nh),
        out_shape=jax.ShapeDtypeStruct(tokens.shape, tokens.dtype),
        in_specs=[
            vmem,
            vmem,
            anywhere,
            anywhere,
            vmem,
            vmem,
            vmem,
            vmem,
            anywhere,
            vmem,
            anywhere,
            anywhere,
        ],
        out_specs=vmem,
        scratch_shapes=scratch,
        compiler_params=pltpu.CompilerParams(
            collective_id=0, has_side_effects=True, vmem_limit_bytes=56 * 2**20
        ),
        name="layer",
    )(
        tokens,
        input_norm_gain.reshape(1, -1),
        jnp.transpose(query_key_value_weight, (1, 0, 2)),
        forget_gate_weight,
        jnp.transpose(convolution_filter_taps, (0, 2, 1, 3)),
        slot_forget_rate,
        extra_forget_log,
        head_norm_gain,
        output_projection_weight,
        feedforward_norm_gain.reshape(1, -1),
        up_projection_weight,
        down_projection_weight,
    )


def solution(mesh):
    in_specs = (
        P(None, "seq", "head"),
        P(),
        P(None, None, "head"),
        P(None, "head"),
        P(None, None, None, "head"),
        P("head", None),
        P(None, "seq"),
        P("head", None),
        P("head", None),
        P(),
        P(None, "head"),
        P("head", None),
    )
    out_specs = P(None, "seq", "head")
    return jax.shard_map(
        functools.partial(local, mesh.shape["seq"], mesh.shape["head"]),
        mesh=mesh,
        in_specs=in_specs,
        out_specs=out_specs,
        check_vma=False,
    )
```

```python
import functools

import jax
import jax.numpy as jnp
from jax import lax
from jax.experimental import pallas as pl
from jax.experimental.pallas import tpu as pltpu
from jax.sharding import PartitionSpec as P

SPAN = 64
HALO = 16
PIECES = 4
EPSILON = 1e-06
MESH = pl.DeviceIdType.MESH
F32 = jnp.float32
BF16 = jnp.bfloat16


def mm(a, b, ca=1, cb=0):
    return lax.dot_general(a, b, (((ca,), (cb,)), ((), ())), preferred_element_type=F32)


def split_mm(ones, values, count):
    total, rest = None, values
    for _ in range(count):
        part = rest.astype(BF16)
        rest = rest - part.astype(F32)
        term = mm(ones, part)
        total = term if total is None else total + term
    return total


def mm_split(values, ones, count):
    total, rest = None, values
    for _ in range(count):
        part = rest.astype(BF16)
        rest = rest - part.astype(F32)
        term = mm(part, ones)
        total = term if total is None else total + term
    return total


def one_minus_exp(x):
    series = 1.0 + x * (1 / 2 + x * (1 / 6 + x * (1 / 24 + x * (1 / 120 + x * (1 / 720)))))
    return jnp.where(x > -0.25, -x * series, 1.0 - jnp.exp(x))


def iota(shape, dim):
    return lax.broadcasted_iota(jnp.int32, shape, dim)


class Gather:
    def __init__(self, hx, nh, seq, block, send, recv, direct=False):
        self.hx, self.seq, self.block, self.send, self.recv = hx, seq, block, send, recv
        self.direct = direct
        self.masks = []
        m = nh // 2
        while m:
            self.masks.append(m)
            m //= 2
        self.nh = nh
        self.got = {0}

    def copy(self, o, m):
        ref = self.block(self.hx(o))
        return pltpu.make_async_remote_copy(
            src_ref=ref,
            dst_ref=ref,
            send_sem=self.send.at[o ^ m],
            recv_sem=self.recv.at[o ^ m],
            device_id=(self.seq, self.hx(m)),
            device_id_type=MESH,
        )

    def arrive(self, o):
        if o not in self.got:
            ref = self.block(self.hx(o))
            pltpu.make_async_remote_copy(
                src_ref=ref,
                dst_ref=ref,
                send_sem=self.send.at[o],
                recv_sem=self.recv.at[o],
                device_id=(self.seq, self.hx(1)),
                device_id_type=MESH,
            ).wait_recv()
            self.got.add(o)

    def start(self):
        for m in range(1, self.nh) if self.direct else self.masks:
            self.copy(0, m).start()

    def forward(self):
        if self.direct:
            return
        have = [0]
        for m in self.masks:
            for o in have:
                if o:
                    self.arrive(o)
                    self.copy(o, m).start()
            have = have + [o ^ m for o in have]

    def finish(self):
        for o in range(1, self.nh):
            self.arrive(o)

    def drain(self):
        if self.direct:
            for m in range(1, self.nh):
                self.copy(0, m).wait_send()
            return
        have = [0]
        for m in self.masks:
            for o in have:
                self.copy(o, m).wait_send()
            have = have + [o ^ m for o in have]


def kernel(
    n,
    nh,
    tok,
    gain1,
    wqkv,
    wgate,
    taps,
    rate,
    extra,
    hgain,
    wo,
    gain2,
    wup,
    wdown,
    out,
    xg,
    wq_v,
    wg_v,
    wo_v,
    up_v,
    dn_v,
    nb,
    pj,
    qkv,
    growth_v,
    shrink_v,
    score_v,
    local_v,
    before_v,
    apost,
    arecv,
    fpost,
    frecv,
    cin,
    csend,
    crecv,
    sst,
    begin,
    pair_v,
    pairf_v,
    ag,
    res,
    pf,
    pb,
    rb,
    lsem,
    tok_s,
    tok_r,
    halo_s,
    halo_r,
    wo_s,
    wo_r,
    sib_s,
    sib_r,
    ch_s,
    ch_r,
    st_s,
    st_r,
    at_s,
    at_r,
    rs_s,
    rs_r,
):
    batch, rows, width = tok.shape
    heads, hd = hgain.shape
    spans = rows // SPAN
    s = lax.axis_index("seq")
    h = lax.axis_index("head")

    def hx(o):
        r, bit = h, 1
        while bit <= o:
            if o & bit:
                r = r + bit - 2 * bit * lax.rem(lax.div(r, bit), 2)
            bit *= 2
        return r

    def ring(d):
        return lax.rem(s + d + n, n)

    odd = lax.rem(s, 2)
    pair = lax.div(s, 2)
    pairs = n // 2
    sibling = s + 1 - 2 * odd

    loads = [
        pltpu.make_async_copy(wqkv, wq_v, lsem.at[0]),
        pltpu.make_async_copy(wgate, wg_v, lsem.at[1]),
        pltpu.make_async_copy(wo, wo_v.at[h], lsem.at[2]),
        pltpu.make_async_copy(wup, up_v, lsem.at[3]),
        pltpu.make_async_copy(wdown, dn_v, lsem.at[4]),
    ]
    for load in loads:
        load.start()

    barrier = pltpu.get_barrier_semaphore()
    greeted = [(s, hx(o)) for o in range(1, nh)]
    greeted += [(ring(d), hx(o)) for d in (-1, 1) for o in range(nh)]
    greeted += [(ring(d), h) for d in (-2, 2)]
    for device in greeted:
        pl.semaphore_signal(barrier, inc=1, device_id=device, device_id_type=MESH)
    xg[h, :, HALO : HALO + rows, :] = tok[...]
    cin[...] = jnp.zeros_like(cin)
    pl.semaphore_wait(barrier, len(greeted))

    tokens = Gather(hx, nh, s, lambda i: xg.at[i, :, HALO : HALO + rows, :], tok_s, tok_r)
    tokens.start()
    halos = []
    for o in range(nh):
        for side in (0, 1):
            src = xg.at[h, :, rows : rows + HALO, :] if side == 0 else xg.at[h, :, HALO : 2 * HALO, :]
            at = 0 if side == 0 else HALO + rows
            halos.append(
                pltpu.make_async_remote_copy(
                    src_ref=src,
                    dst_ref=xg.at[h, :, at : at + HALO, :],
                    send_sem=halo_s.at[side, o],
                    recv_sem=halo_r.at[side, o],
                    device_id=(ring(1) if side == 0 else ring(-1), hx(o)),
                    device_id_type=MESH,
                )
            )
    for copy in halos:
        copy.start()
    tokens.forward()
    piece = width // PIECES
    projection = [
        Gather(
            hx, nh, s, lambda i, c=c: wo_v.at[i, c * piece : (c + 1) * piece, :], wo_s.at[c], wo_r.at[c]
        )
        for c in range(PIECES)
    ]
    loads[2].wait()
    projection[0].start()
    projection[1].start()
    tokens.finish()
    for copy in halos:
        copy.wait_recv()

    tall = rows + 2 * HALO
    row_at = iota((tall, 1), 0)
    inside = jnp.logical_and(
        jnp.logical_or(row_at >= HALO, s > 0),
        jnp.logical_or(row_at < HALO + rows, s < n - 1),
    )
    for b in range(batch):
        parts = [xg[j, b].astype(F32) for j in range(nh)]
        square = parts[0] * parts[0]
        for part in parts[1:]:
            square = square + part * part
        mean = jnp.sum(square, axis=1, keepdims=True) / (nh * width)
        scale = jnp.where(inside, lax.rsqrt(mean + EPSILON), 0.0)
        for j in range(nh):
            cols = slice(j * width, (j + 1) * width)
            nb[b, :, cols] = (parts[j] * scale * gain1[:, cols]).astype(BF16)

    loads[0].wait()
    loads[1].wait()
    normed = nb[...].reshape(batch * tall, nh * width)

    def project(i):
        made = mm(normed, wq_v[i]).astype(BF16).astype(F32)
        pj[i] = made.reshape(batch, tall, width)

    def convolve(d, i, b):
        acc = None
        for j in range(4):
            first = HALO + j if d else HALO - j
            term = taps[d, i, j : j + 1, :] * pj[i, b, first : first + rows, :]
            acc = term if acc is None else acc + term
        qkv[d, i, b] = (acc * jax.nn.sigmoid(acc)).astype(BF16)

    project(1)
    project(2)

    lanes = iota((1, width), 1)
    lane_head = lax.div(lanes, hd)
    block_mask = (
        lax.div(iota((width, width), 0), hd) == lax.div(iota((width, width), 1), hd)
    ).astype(F32).astype(BF16)
    causal_t = iota((SPAN, width), 0)
    causal_j = lax.rem(iota((SPAN, width), 1), SPAN)
    causal = [(causal_t >= causal_j).astype(F32), (causal_t <= causal_j).astype(F32)]
    big_t, big_j = iota((rows, rows), 0), iota((rows, rows), 1)
    same = lax.div(big_t, SPAN) == lax.div(big_j, SPAN)
    running = jnp.logical_and(same, big_t >= big_j).astype(F32).astype(BF16)
    rate_row = jnp.concatenate([rate[i : i + 1, :] for i in range(heads)], axis=1)
    gain_row = jnp.concatenate([hgain[i : i + 1, :] for i in range(heads)], axis=1)

    def expand(x):
        return jnp.concatenate([x] * heads, axis=0) * block_mask

    def compact(x):
        total = None
        for i in range(heads):
            term = jnp.where(lane_head == i, x[i * hd : (i + 1) * hd], 0.0)
            total = term if total is None else total + term
        return total

    decays = []
    for b in range(batch):
        logits = mm(nb[b, HALO : HALO + rows, :], wg_v[...])
        column = jnp.sum(
            jnp.where(big_t == big_j, extra[b : b + 1, :], 0.0), axis=1, keepdims=True
        )
        decays.append(-2.0 * rate_row * jax.nn.sigmoid(logits) - column)
    prefixes = split_mm(running, jnp.concatenate(decays, axis=1), 2)
    prefixes = [prefixes[:, b * width : (b + 1) * width] for b in range(batch)]
    inflows = [one_minus_exp(x) for x in decays]
    totals = [
        [prefixes[b][(g + 1) * SPAN - 1 : (g + 1) * SPAN] for g in range(spans)]
        for b in range(batch)
    ]

    def sib_copies(d):
        return [
            pltpu.make_async_remote_copy(
                src_ref=src,
                dst_ref=dst,
                send_sem=sib_s.at[d, k],
                recv_sem=sib_r.at[d, k],
                device_id=(sibling, h),
                device_id_type=MESH,
            )
            for k, (src, dst) in enumerate(
                ((apost.at[d, 1 - odd], arecv.at[d]), (fpost.at[d], frecv.at[d]))
            )
        ]

    fpost[...] = jnp.zeros_like(fpost)
    order = [list(range(spans)), list(range(spans))[::-1]]
    cells = [(b, g, slice(g * SPAN, (g + 1) * SPAN)) for b in range(batch) for g in range(spans)]
    for d in (0, 1):
        remain = {}
        for b, g, span in cells:
            cum, ld = prefixes[b][span], decays[b][span]
            if d:
                cum = totals[b][g] - cum + ld
            shrink = jnp.exp(-cum) * inflows[b][span]
            growth_v[d, b, span, :] = jnp.exp(cum)
            shrink_v[d, b, span, :] = shrink.astype(BF16)
            remain[b, g] = (jnp.exp(totals[b][g]) * shrink).astype(BF16)
        for b in range(batch):
            for i in (1, 2):
                convolve(d, i, b)
        fresh = {
            (b, g, i): mm(qkv[d, i, b, span, :], remain[b, g], 0, 0)
            for b, g, span in cells
            for i in (1, 2)
        }
        for b in range(batch):
            state = jnp.zeros((2 * hd, width), F32)
            past = jnp.zeros((1, width), F32)
            for g in order[d]:
                local_v[d, b, g] = state
                before_v[d, b, g : g + 1, :] = jnp.exp(past)
                new = jnp.concatenate([compact(fresh[b, g, i]) for i in (1, 2)], axis=0)
                state = jnp.exp(totals[b][g]) * state + new
                past = past + totals[b][g]
            apost[d, 0, b] = state[:hd].astype(BF16)
            apost[d, 1, b] = state[hd:].astype(BF16)
            fpost[d, b : b + 1, :] = jnp.exp(past)
        for copy in sib_copies(d):
            copy.start()

    project(0)
    for d in (0, 1):
        for b in range(batch):
            convolve(d, 0, b)

    def local_scores():
        both = [(d, b, span) for d in (0, 1) for b, g, span in cells]
        inter = [
            mm(qkv[d, 0, b, span, :], expand(qkv[d, 1, b, span, :]), 1, 1) for d, b, span in both
        ]
        inter = [(x * causal[d]).astype(BF16) for x, (d, b, span) in zip(inter, both)]
        made = [mm(x, expand(shrink_v[d, b, span, :])) for x, (d, b, span) in zip(inter, both)]
        for x, (d, b, span) in zip(made, both):
            score_v[d, b, span, :] = x

    later = [odd.astype(F32), 1.0 - odd.astype(F32)]
    for d in (0, 1):
        for copy in sib_copies(d):
            copy.wait_recv()
        for b in range(batch):
            mine, other = apost[d, odd, b].astype(F32), arecv[d, b].astype(F32)
            fm, fo = fpost[d, b : b + 1, :], frecv[d, b : b + 1, :]
            pair_v[d, b] = later[d] * (fm * other + mine) + (1.0 - later[d]) * (fo * mine + other)
            pairf_v[d, b : b + 1, :] = fm * fo

    first_pair = [pair == 0, pair == pairs - 1]
    last_pair = [pair == pairs - 1, pair == 0]

    def hop_copy(d, b):
        return pltpu.make_async_remote_copy(
            src_ref=csend.at[d, b],
            dst_ref=crecv.at[d, b],
            send_sem=ch_s.at[d, b],
            recv_sem=ch_r.at[d, b],
            device_id=(ring(-2) if d else ring(2), h),
            device_id_type=MESH,
        )

    def start_copy(d, b):
        return pltpu.make_async_remote_copy(
            src_ref=sst.at[d, b],
            dst_ref=begin.at[d, odd, b],
            send_sem=st_s.at[d, b],
            recv_sem=st_r.at[d, b],
            device_id=(sibling, h),
            device_id_type=MESH,
        )

    def await_start(d, b):
        pltpu.make_async_remote_copy(
            src_ref=sst.at[d, b],
            dst_ref=begin.at[d, 1 - odd, b],
            send_sem=st_s.at[d, b],
            recv_sem=st_r.at[d, b],
            device_id=(sibling, h),
            device_id_type=MESH,
        ).wait_recv()

    def pass_on(d, b):
        csend[d, b] = (pairf_v[d, b : b + 1, :] * cin[d, b] + pair_v[d, b]).astype(BF16)
        hop_copy(d, b).start()

    def open_chain(d):
        @pl.when(jnp.logical_and(first_pair[d], jnp.logical_not(last_pair[d])))
        def _():
            for b in range(batch):
                pass_on(d, b)

    def hop(d):
        for b in range(batch):

            @pl.when(jnp.logical_not(first_pair[d]))
            def _():
                hop_copy(d, b).wait_recv()
                cin[d, b] = crecv[d, b].astype(F32)

            @pl.when(jnp.logical_not(jnp.logical_or(first_pair[d], last_pair[d])))
            def _():
                pass_on(d, b)

            carry = cin[d, b]
            fm, fo = fpost[d, b : b + 1, :], frecv[d, b : b + 1, :]
            mine, other = apost[d, odd, b].astype(F32), arecv[d, b].astype(F32)
            theirs = (1.0 - later[d]) * (fm * carry + mine) + later[d] * carry
            sst[d, b] = theirs.astype(BF16)
            start_copy(d, b).start()
            own = later[d] * (fo * carry + other) + (1.0 - later[d]) * carry
            begin[d, odd, b] = own.astype(BF16)

    lower = 2 * pair < pairs
    open_chain(0)
    open_chain(1)
    projection[2].start()
    local_scores()

    @pl.when(lower)
    def _():
        hop(0)

    @pl.when(jnp.logical_not(lower))
    def _():
        hop(1)

    projection[3].start()

    @pl.when(lower)
    def _():
        hop(1)

    @pl.when(jnp.logical_not(lower))
    def _():
        hop(0)

    for member in projection[:2]:
        member.forward()

    attends = [
        Gather(hx, nh, s, lambda i, b=b: ag.at[i, b], at_s.at[b], at_r.at[b], b + 1 < batch)
        for b in range(batch)
    ]
    group = min(width, 128)

    def head_max(x):
        tops = []
        for c in range(0, width, group):
            part, head = x[:, c : c + group], lane_head[:, c : c + group]
            top = None
            for i in range(c // hd, (c + group) // hd):
                best = jnp.max(jnp.where(head == i, part, -jnp.inf), axis=1, keepdims=True)
                top = best if top is None else jnp.where(head == i, best, top)
            tops.append(jnp.broadcast_to(top, part.shape))
        return jnp.concatenate(tops, axis=1)

    def stacked(xs):
        sums = mm(jnp.concatenate([x.astype(BF16) for x in xs], axis=0), block_mask)
        return [sums[i * SPAN : (i + 1) * SPAN] for i in range(len(xs))]

    for b in range(batch):
        for d in (0, 1):
            await_start(d, b)
        blocks = [(d, g, slice(g * SPAN, (g + 1) * SPAN)) for g in range(spans) for d in (0, 1)]
        keys, values = [
            [
                (
                    before_v[d, b, g : g + 1, :] * begin[d, i, b].astype(F32)
                    + local_v[d, b, g, i * hd : (i + 1) * hd, :]
                ).astype(BF16)
                for d, g, span in blocks
            ]
            for i in (0, 1)
        ]
        growth = [growth_v[d, b, span, :] for d, g, span in blocks]
        scores = [mm(qkv[d, 0, b, span, :], expand(k)) for (d, g, span), k in zip(blocks, keys)]
        scores = [
            w * (score_v[d, b, span, :] + x) for (d, g, span), x, w in zip(blocks, scores, growth)
        ]
        power = [jnp.exp(x - head_max(x)) for x in scores]
        norm = stacked(power)
        weighted = [(x / y * w).astype(BF16) for x, y, w in zip(power, norm, growth)]
        mixing = [
            mm(x, expand(shrink_v[d, b, span, :]), 1, 1) for (d, g, span), x in zip(blocks, weighted)
        ]
        mixing = [(x * causal[d]).astype(BF16) for (d, g, span), x in zip(blocks, mixing)]
        carried = [mm(x, expand(v), 1, 1) for x, v in zip(weighted, values)]
        made = [
            x + mm(y, expand(qkv[d, 2, b, span, :]))
            for (d, g, span), x, y in zip(blocks, carried, mixing)
        ]
        mean = [x / hd for x in stacked([x * x for x in made])]
        made = [x * lax.rsqrt(y + EPSILON) * gain_row for x, y in zip(made, mean)]
        for g in range(spans):
            span = slice(g * SPAN, (g + 1) * SPAN)
            ag[h, b, span, :] = (made[2 * g] + made[2 * g + 1]).astype(BF16)
        attends[b].start()
        if b == 0:
            for member in projection[2:]:
                member.forward()
    attends[0].forward()

    for member in projection:
        member.finish()
    loads[3].wait()
    loads[4].wait()

    masks = [1 << i for i in range(nh.bit_length() - 1)]

    def rs_copy(b, o, m):
        return pltpu.make_async_remote_copy(
            src_ref=pb.at[hx(o), b],
            dst_ref=rb.at[o ^ m, m.bit_length() - 1, b],
            send_sem=rs_s.at[b, o],
            recv_sem=rs_r.at[b, o],
            device_id=(s, hx(m)),
            device_id_type=MESH,
        )

    leaving = sorted(range(nh), key=lambda o: [-((o >> k) & 1) for k in range(len(masks))])

    def level(o):
        return next((k for k, m in enumerate(masks) if o & m), len(masks))

    def settle(b, o):
        total = pf[hx(o), b]
        for k in range(level(o)):
            rs_copy(b, o ^ masks[k], masks[k]).wait_recv()
            total = total + rb[o, k, b].astype(F32)
        if o:
            pb[hx(o), b] = total.astype(BF16)
            rs_copy(b, o, masks[level(o)]).start()
        else:
            out[b] = (res[h, b].astype(F32) + total).astype(BF16)

    wo_all = wo_v[...].reshape(nh * width, nh * width)
    for b in range(batch):
        attends[b].finish()
        attention = jnp.concatenate([ag[j, b] for j in range(nh)], axis=1)
        whole = jnp.concatenate([xg[j, b, HALO : HALO + rows, :] for j in range(nh)], axis=1)
        residual = (whole.astype(F32) + mm(attention, wo_all)).astype(BF16)
        wide = residual.astype(F32)
        for j in range(nh):
            res[j, b] = residual[:, j * width : (j + 1) * width]
        mean = jnp.mean(wide * wide, axis=1, keepdims=True)
        mlp_in = (wide * lax.rsqrt(mean + EPSILON) * gain2[...]).astype(BF16)
        hidden = jax.nn.gelu(mm(mlp_in, up_v[...])).astype(BF16)
        if b + 1 < batch:
            attends[b + 1].forward()
        if b:
            for o in leaving:
                if 0 < level(o) < len(masks):
                    settle(b - 1, o)
        for o in leaving:
            cols = pl.ds(pl.multiple_of(hx(o) * width, width), width)
            made = mm(hidden, dn_v[:, cols])
            if level(o) == 0 and o:
                pb[hx(o), b] = made.astype(BF16)
                rs_copy(b, o, masks[0]).start()
            else:
                pf[hx(o), b] = made
                if o and b == batch - 1:
                    settle(b, o)
    for b in range(batch):
        settle(b, 0)

    tokens.drain()
    for member in projection:
        member.drain()
    for copy in halos:
        copy.wait_send()
    for d in (0, 1):
        for copy in sib_copies(d):
            copy.wait_send()

        @pl.when(jnp.logical_not(last_pair[d]))
        def _():
            for b in range(batch):
                hop_copy(d, b).wait_send()

        for b in range(batch):
            start_copy(d, b).wait_send()

    for b in range(batch):
        attends[b].drain()
        for o in range(1, nh):
            rs_copy(b, o, masks[level(o)]).wait_send()


def local(
    n,
    nh,
    tokens,
    input_norm_gain,
    query_key_value_weight,
    forget_gate_weight,
    convolution_filter_taps,
    slot_forget_rate,
    extra_forget_log,
    head_norm_gain,
    output_projection_weight,
    feedforward_norm_gain,
    up_projection_weight,
    down_projection_weight,
):
    batch, rows, width = tokens.shape
    depth = nh * width
    hidden = up_projection_weight.shape[1]
    spans = rows // SPAN
    hd = head_norm_gain.shape[1]
    tall = rows + 2 * HALO
    vmem = pl.BlockSpec(memory_space=pltpu.VMEM)
    anywhere = pl.BlockSpec(memory_space=pl.ANY)
    dma = pltpu.SemaphoreType.DMA
    bits = nh.bit_length() - 1
    scratch = [
        pltpu.VMEM((nh, batch, tall, width), BF16),
        pltpu.VMEM((3, depth, width), BF16),
        pltpu.VMEM((depth, width), BF16),
        pltpu.VMEM((nh, width, depth), BF16),
        pltpu.VMEM((depth, hidden), BF16),
        pltpu.VMEM((hidden, depth), BF16),
        pltpu.VMEM((batch, tall, depth), BF16),
        pltpu.VMEM((3, batch, tall, width), F32),
        pltpu.VMEM((2, 3, batch, rows, width), BF16),
        pltpu.VMEM((2, batch, rows, width), F32),
        pltpu.VMEM((2, batch, rows, width), BF16),
        pltpu.VMEM((2, batch, rows, width), F32),
        pltpu.VMEM((2, batch, spans, 2 * hd, width), F32),
        pltpu.VMEM((2, batch, spans, width), F32),
        pltpu.VMEM((2, 2, batch, hd, width), BF16),
        pltpu.VMEM((2, batch, hd, width), BF16),
        pltpu.VMEM((2, 8 * pl.cdiv(batch, 8), width), F32),
        pltpu.VMEM((2, 8 * pl.cdiv(batch, 8), width), F32),
        pltpu.VMEM((2, batch, hd, width), F32),
        pltpu.VMEM((2, batch, hd, width), BF16),
        pltpu.VMEM((2, batch, hd, width), BF16),
        pltpu.VMEM((2, batch, hd, width), BF16),
        pltpu.VMEM((2, 2, batch, hd, width), BF16),
        pltpu.VMEM((2, batch, hd, width), F32),
        pltpu.VMEM((2, batch, width), F32),
        pltpu.VMEM((nh, batch, rows, width), BF16),
        pltpu.VMEM((nh, batch, rows, width), BF16),
        pltpu.VMEM((nh, batch, rows, width), F32),
        pltpu.VMEM((nh, batch, rows, width), BF16),
        pltpu.VMEM((nh, bits, batch, rows, width), BF16),
        dma((5,)),
        dma((nh,)),
        dma((nh,)),
        dma((2, nh)),
        dma((2, nh)),
        dma((PIECES, nh)),
        dma((PIECES, nh)),
        dma((2, 2)),
        dma((2, 2)),
        dma((2, batch)),
        dma((2, batch)),
        dma((2, batch)),
        dma((2, batch)),
        dma((batch, nh)),
        dma((batch, nh)),
        dma((batch, nh)),
        dma((batch, nh)),
    ]
    return pl.pallas_call(
        functools.partial(kernel, n, nh),
        out_shape=jax.ShapeDtypeStruct(tokens.shape, tokens.dtype),
        in_specs=[
            vmem,
            vmem,
            anywhere,
            anywhere,
            vmem,
            vmem,
            vmem,
            vmem,
            anywhere,
            vmem,
            anywhere,
            anywhere,
        ],
        out_specs=vmem,
        scratch_shapes=scratch,
        compiler_params=pltpu.CompilerParams(
            collective_id=0, has_side_effects=True, vmem_limit_bytes=56 * 2**20
        ),
        name="layer",
    )(
        tokens,
        input_norm_gain.reshape(1, -1),
        jnp.transpose(query_key_value_weight, (1, 0, 2)),
        forget_gate_weight,
        jnp.transpose(convolution_filter_taps, (0, 2, 1, 3)),
        slot_forget_rate,
        extra_forget_log,
        head_norm_gain,
        output_projection_weight,
        feedforward_norm_gain.reshape(1, -1),
        up_projection_weight,
        down_projection_weight,
    )


def solution(mesh):
    in_specs = (
        P(None, "seq", "head"),
        P(),
        P(None, None, "head"),
        P(None, "head"),
        P(None, None, None, "head"),
        P("head", None),
        P(None, "seq"),
        P("head", None),
        P("head", None),
        P(),
        P(None, "head"),
        P("head", None),
    )
    out_specs = P(None, "seq", "head")
    return jax.shard_map(
        functools.partial(local, mesh.shape["seq"], mesh.shape["head"]),
        mesh=mesh,
        in_specs=in_specs,
        out_specs=out_specs,
        check_vma=False,
    )
```

```python
import functools

import jax
import jax.numpy as jnp
from jax import lax
from jax.experimental import pallas as pl
from jax.experimental.pallas import tpu as pltpu
from jax.sharding import PartitionSpec as P

SPAN = 64
HALO = 16
PIECES = 4
EPSILON = 1e-06
MESH = pl.DeviceIdType.MESH
F32 = jnp.float32
BF16 = jnp.bfloat16


def mm(a, b, ca=1, cb=0):
    return lax.dot_general(a, b, (((ca,), (cb,)), ((), ())), preferred_element_type=F32)


def split_mm(ones, values, count):
    total, rest = None, values
    for _ in range(count):
        part = rest.astype(BF16)
        rest = rest - part.astype(F32)
        term = mm(ones, part)
        total = term if total is None else total + term
    return total


def mm_split(values, ones, count):
    total, rest = None, values
    for _ in range(count):
        part = rest.astype(BF16)
        rest = rest - part.astype(F32)
        term = mm(part, ones)
        total = term if total is None else total + term
    return total


def one_minus_exp(x):
    series = 1.0 + x * (1 / 2 + x * (1 / 6 + x * (1 / 24 + x * (1 / 120 + x * (1 / 720)))))
    return jnp.where(x > -0.25, -x * series, 1.0 - jnp.exp(x))


def iota(shape, dim):
    return lax.broadcasted_iota(jnp.int32, shape, dim)


class Gather:
    def __init__(self, hx, nh, seq, block, send, recv, direct=False):
        self.hx, self.seq, self.block, self.send, self.recv = hx, seq, block, send, recv
        self.direct = direct
        self.masks = []
        m = nh // 2
        while m:
            self.masks.append(m)
            m //= 2
        self.nh = nh
        self.got = {0}

    def copy(self, o, m):
        ref = self.block(self.hx(o))
        return pltpu.make_async_remote_copy(
            src_ref=ref,
            dst_ref=ref,
            send_sem=self.send.at[o ^ m],
            recv_sem=self.recv.at[o ^ m],
            device_id=(self.seq, self.hx(m)),
            device_id_type=MESH,
        )

    def arrive(self, o):
        if o not in self.got:
            ref = self.block(self.hx(o))
            pltpu.make_async_remote_copy(
                src_ref=ref,
                dst_ref=ref,
                send_sem=self.send.at[o],
                recv_sem=self.recv.at[o],
                device_id=(self.seq, self.hx(1)),
                device_id_type=MESH,
            ).wait_recv()
            self.got.add(o)

    def start(self):
        for m in range(1, self.nh) if self.direct else self.masks:
            self.copy(0, m).start()

    def forward(self):
        if self.direct:
            return
        have = [0]
        for m in self.masks:
            for o in have:
                if o:
                    self.arrive(o)
                    self.copy(o, m).start()
            have = have + [o ^ m for o in have]

    def finish(self):
        for o in range(1, self.nh):
            self.arrive(o)

    def drain(self):
        if self.direct:
            for m in range(1, self.nh):
                self.copy(0, m).wait_send()
            return
        have = [0]
        for m in self.masks:
            for o in have:
                self.copy(o, m).wait_send()
            have = have + [o ^ m for o in have]


def kernel(
    n,
    nh,
    tok,
    gain1,
    wqkv,
    wgate,
    taps,
    rate,
    extra,
    hgain,
    wo,
    gain2,
    wup,
    wdown,
    out,
    xg,
    wq_v,
    wg_v,
    wo_v,
    up_v,
    dn_v,
    nb,
    pj,
    qkv,
    growth_v,
    shrink_v,
    score_v,
    local_v,
    before_v,
    apost,
    arecv,
    fpost,
    frecv,
    cin,
    csend,
    crecv,
    sst,
    begin,
    pair_v,
    pairf_v,
    ag,
    res,
    pf,
    pb,
    rb,
    lsem,
    tok_s,
    tok_r,
    halo_s,
    halo_r,
    wo_s,
    wo_r,
    sib_s,
    sib_r,
    ch_s,
    ch_r,
    st_s,
    st_r,
    at_s,
    at_r,
    rs_s,
    rs_r,
):
    batch, rows, width = tok.shape
    heads, hd = hgain.shape
    spans = rows // SPAN
    s = lax.axis_index("seq")
    h = lax.axis_index("head")

    def hx(o):
        r, bit = h, 1
        while bit <= o:
            if o & bit:
                r = r + bit - 2 * bit * lax.rem(lax.div(r, bit), 2)
            bit *= 2
        return r

    def ring(d):
        return lax.rem(s + d + n, n)

    odd = lax.rem(s, 2)
    pair = lax.div(s, 2)
    pairs = n // 2
    sibling = s + 1 - 2 * odd

    loads = [
        pltpu.make_async_copy(wqkv, wq_v, lsem.at[0]),
        pltpu.make_async_copy(wgate, wg_v, lsem.at[1]),
        pltpu.make_async_copy(wo, wo_v.at[h], lsem.at[2]),
        pltpu.make_async_copy(wup, up_v, lsem.at[3]),
        pltpu.make_async_copy(wdown, dn_v, lsem.at[4]),
    ]
    for load in loads:
        load.start()

    barrier = pltpu.get_barrier_semaphore()
    greeted = [(s, hx(o)) for o in range(1, nh)]
    greeted += [(ring(d), hx(o)) for d in (-1, 1) for o in range(nh)]
    greeted += [(ring(d), h) for d in (-2, 2)]
    for device in greeted:
        pl.semaphore_signal(barrier, inc=1, device_id=device, device_id_type=MESH)
    xg[h, :, HALO : HALO + rows, :] = tok[...]
    cin[...] = jnp.zeros_like(cin)
    pl.semaphore_wait(barrier, len(greeted))

    tokens = Gather(hx, nh, s, lambda i: xg.at[i, :, HALO : HALO + rows, :], tok_s, tok_r)
    tokens.start()
    halos = []
    for o in range(nh):
        for side in (0, 1):
            src = xg.at[h, :, rows : rows + HALO, :] if side == 0 else xg.at[h, :, HALO : 2 * HALO, :]
            at = 0 if side == 0 else HALO + rows
            halos.append(
                pltpu.make_async_remote_copy(
                    src_ref=src,
                    dst_ref=xg.at[h, :, at : at + HALO, :],
                    send_sem=halo_s.at[side, o],
                    recv_sem=halo_r.at[side, o],
                    device_id=(ring(1) if side == 0 else ring(-1), hx(o)),
                    device_id_type=MESH,
                )
            )
    for copy in halos:
        copy.start()
    tokens.forward()
    piece = width // PIECES
    projection = [
        Gather(
            hx, nh, s, lambda i, c=c: wo_v.at[i, c * piece : (c + 1) * piece, :], wo_s.at[c], wo_r.at[c]
        )
        for c in range(PIECES)
    ]
    loads[2].wait()
    projection[0].start()
    projection[1].start()
    tokens.finish()
    for copy in halos:
        copy.wait_recv()

    tall = rows + 2 * HALO
    row_at = iota((tall, 1), 0)
    inside = jnp.logical_and(
        jnp.logical_or(row_at >= HALO, s > 0),
        jnp.logical_or(row_at < HALO + rows, s < n - 1),
    )
    for b in range(batch):
        parts = [xg[j, b].astype(F32) for j in range(nh)]
        square = parts[0] * parts[0]
        for part in parts[1:]:
            square = square + part * part
        mean = jnp.sum(square, axis=1, keepdims=True) / (nh * width)
        scale = jnp.where(inside, lax.rsqrt(mean + EPSILON), 0.0)
        for j in range(nh):
            cols = slice(j * width, (j + 1) * width)
            nb[b, :, cols] = (parts[j] * scale * gain1[:, cols]).astype(BF16)

    loads[0].wait()
    loads[1].wait()
    normed = nb[...].reshape(batch * tall, nh * width)

    def project(i):
        made = mm(normed, wq_v[i]).astype(BF16).astype(F32)
        pj[i] = made.reshape(batch, tall, width)

    def convolve(d, i, b):
        acc = None
        for j in range(4):
            first = HALO + j if d else HALO - j
            term = taps[d, i, j : j + 1, :] * pj[i, b, first : first + rows, :]
            acc = term if acc is None else acc + term
        qkv[d, i, b] = (acc * jax.nn.sigmoid(acc)).astype(BF16)

    project(1)
    project(2)

    lanes = iota((1, width), 1)
    lane_head = lax.div(lanes, hd)
    block_mask = (
        lax.div(iota((width, width), 0), hd) == lax.div(iota((width, width), 1), hd)
    ).astype(F32).astype(BF16)
    causal_t = iota((SPAN, width), 0)
    causal_j = lax.rem(iota((SPAN, width), 1), SPAN)
    causal = [(causal_t >= causal_j).astype(F32), (causal_t <= causal_j).astype(F32)]
    big_t, big_j = iota((rows, rows), 0), iota((rows, rows), 1)
    same = lax.div(big_t, SPAN) == lax.div(big_j, SPAN)
    running = jnp.logical_and(same, big_t >= big_j).astype(F32).astype(BF16)
    rate_row = jnp.concatenate([rate[i : i + 1, :] for i in range(heads)], axis=1)
    gain_row = jnp.concatenate([hgain[i : i + 1, :] for i in range(heads)], axis=1)

    def expand(x):
        return jnp.concatenate([x] * heads, axis=0) * block_mask

    def compact(x):
        total = None
        for i in range(heads):
            term = jnp.where(lane_head == i, x[i * hd : (i + 1) * hd], 0.0)
            total = term if total is None else total + term
        return total

    decays = []
    for b in range(batch):
        logits = mm(nb[b, HALO : HALO + rows, :], wg_v[...])
        column = jnp.sum(
            jnp.where(big_t == big_j, extra[b : b + 1, :], 0.0), axis=1, keepdims=True
        )
        decays.append(-2.0 * rate_row * jax.nn.sigmoid(logits) - column)
    prefixes = split_mm(running, jnp.concatenate(decays, axis=1), 2)
    prefixes = [prefixes[:, b * width : (b + 1) * width] for b in range(batch)]
    inflows = [one_minus_exp(x) for x in decays]
    totals = [
        [prefixes[b][(g + 1) * SPAN - 1 : (g + 1) * SPAN] for g in range(spans)]
        for b in range(batch)
    ]

    def sib_copies(d):
        return [
            pltpu.make_async_remote_copy(
                src_ref=src,
                dst_ref=dst,
                send_sem=sib_s.at[d, k],
                recv_sem=sib_r.at[d, k],
                device_id=(sibling, h),
                device_id_type=MESH,
            )
            for k, (src, dst) in enumerate(
                ((apost.at[d, 1 - odd], arecv.at[d]), (fpost.at[d], frecv.at[d]))
            )
        ]

    fpost[...] = jnp.zeros_like(fpost)
    order = [list(range(spans)), list(range(spans))[::-1]]
    cells = [(b, g, slice(g * SPAN, (g + 1) * SPAN)) for b in range(batch) for g in range(spans)]
    for d in (0, 1):
        remain = {}
        for b, g, span in cells:
            cum, ld = prefixes[b][span], decays[b][span]
            if d:
                cum = totals[b][g] - cum + ld
            shrink = jnp.exp(-cum) * inflows[b][span]
            growth_v[d, b, span, :] = jnp.exp(cum)
            shrink_v[d, b, span, :] = shrink.astype(BF16)
            remain[b, g] = (jnp.exp(totals[b][g]) * shrink).astype(BF16)
        for b in range(batch):
            for i in (1, 2):
                convolve(d, i, b)
        fresh = {
            (b, g, i): mm(qkv[d, i, b, span, :], remain[b, g], 0, 0)
            for b, g, span in cells
            for i in (1, 2)
        }
        for b in range(batch):
            state = jnp.zeros((2 * hd, width), F32)
            past = jnp.zeros((1, width), F32)
            for g in order[d]:
                local_v[d, b, g] = state
                before_v[d, b, g : g + 1, :] = jnp.exp(past)
                new = jnp.concatenate([compact(fresh[b, g, i]) for i in (1, 2)], axis=0)
                state = jnp.exp(totals[b][g]) * state + new
                past = past + totals[b][g]
            apost[d, 0, b] = state[:hd].astype(BF16)
            apost[d, 1, b] = state[hd:].astype(BF16)
            fpost[d, b : b + 1, :] = jnp.exp(past)
        for copy in sib_copies(d):
            copy.start()

    def local_scores():
        both = [(d, b, span) for d in (0, 1) for b, g, span in cells]
        inter = [
            mm(qkv[d, 0, b, span, :], expand(qkv[d, 1, b, span, :]), 1, 1) for d, b, span in both
        ]
        inter = [(x * causal[d]).astype(BF16) for x, (d, b, span) in zip(inter, both)]
        made = [mm(x, expand(shrink_v[d, b, span, :])) for x, (d, b, span) in zip(inter, both)]
        for x, (d, b, span) in zip(made, both):
            score_v[d, b, span, :] = x

    later = [odd.astype(F32), 1.0 - odd.astype(F32)]

    def join(d):
        for copy in sib_copies(d):
            copy.wait_recv()
        for b in range(batch):
            mine, other = apost[d, odd, b].astype(F32), arecv[d, b].astype(F32)
            fm, fo = fpost[d, b : b + 1, :], frecv[d, b : b + 1, :]
            pair_v[d, b] = later[d] * (fm * other + mine) + (1.0 - later[d]) * (fo * mine + other)
            pairf_v[d, b : b + 1, :] = fm * fo

    first_pair = [pair == 0, pair == pairs - 1]
    last_pair = [pair == pairs - 1, pair == 0]

    def hop_copy(d, b):
        return pltpu.make_async_remote_copy(
            src_ref=csend.at[d, b],
            dst_ref=crecv.at[d, b],
            send_sem=ch_s.at[d, b],
            recv_sem=ch_r.at[d, b],
            device_id=(ring(-2) if d else ring(2), h),
            device_id_type=MESH,
        )

    def start_copy(d, b):
        return pltpu.make_async_remote_copy(
            src_ref=sst.at[d, b],
            dst_ref=begin.at[d, odd, b],
            send_sem=st_s.at[d, b],
            recv_sem=st_r.at[d, b],
            device_id=(sibling, h),
            device_id_type=MESH,
        )

    def await_start(d, b):
        pltpu.make_async_remote_copy(
            src_ref=sst.at[d, b],
            dst_ref=begin.at[d, 1 - odd, b],
            send_sem=st_s.at[d, b],
            recv_sem=st_r.at[d, b],
            device_id=(sibling, h),
            device_id_type=MESH,
        ).wait_recv()

    def pass_on(d, b):
        csend[d, b] = (pairf_v[d, b : b + 1, :] * cin[d, b] + pair_v[d, b]).astype(BF16)
        hop_copy(d, b).start()

    def open_chain(d):
        @pl.when(jnp.logical_and(first_pair[d], jnp.logical_not(last_pair[d])))
        def _():
            for b in range(batch):
                pass_on(d, b)

    def hop(d):
        for b in range(batch):

            @pl.when(jnp.logical_not(first_pair[d]))
            def _():
                hop_copy(d, b).wait_recv()
                cin[d, b] = crecv[d, b].astype(F32)

            @pl.when(jnp.logical_not(jnp.logical_or(first_pair[d], last_pair[d])))
            def _():
                pass_on(d, b)

            carry = cin[d, b]
            fm, fo = fpost[d, b : b + 1, :], frecv[d, b : b + 1, :]
            mine, other = apost[d, odd, b].astype(F32), arecv[d, b].astype(F32)
            theirs = (1.0 - later[d]) * (fm * carry + mine) + later[d] * carry
            sst[d, b] = theirs.astype(BF16)
            start_copy(d, b).start()
            own = later[d] * (fo * carry + other) + (1.0 - later[d]) * carry
            begin[d, odd, b] = own.astype(BF16)

    lower = 2 * pair < pairs
    join(0)
    open_chain(0)
    project(0)
    for d in (0, 1):
        for b in range(batch):
            convolve(d, 0, b)
    join(1)
    open_chain(1)
    projection[2].start()
    local_scores()

    @pl.when(lower)
    def _():
        hop(0)

    @pl.when(jnp.logical_not(lower))
    def _():
        hop(1)

    projection[3].start()

    @pl.when(lower)
    def _():
        hop(1)

    @pl.when(jnp.logical_not(lower))
    def _():
        hop(0)

    for member in projection[:2]:
        member.forward()

    attends = [
        Gather(hx, nh, s, lambda i, b=b: ag.at[i, b], at_s.at[b], at_r.at[b], b + 1 < batch)
        for b in range(batch)
    ]
    group = min(width, 128)

    def head_max(x):
        tops = []
        for c in range(0, width, group):
            part, head = x[:, c : c + group], lane_head[:, c : c + group]
            top = None
            for i in range(c // hd, (c + group) // hd):
                best = jnp.max(jnp.where(head == i, part, -jnp.inf), axis=1, keepdims=True)
                top = best if top is None else jnp.where(head == i, best, top)
            tops.append(jnp.broadcast_to(top, part.shape))
        return jnp.concatenate(tops, axis=1)

    def stacked(xs):
        sums = mm(jnp.concatenate([x.astype(BF16) for x in xs], axis=0), block_mask)
        return [sums[i * SPAN : (i + 1) * SPAN] for i in range(len(xs))]

    for b in range(batch):
        for d in (0, 1):
            await_start(d, b)
        blocks = [(d, g, slice(g * SPAN, (g + 1) * SPAN)) for g in range(spans) for d in (0, 1)]
        keys, values = [
            [
                (
                    before_v[d, b, g : g + 1, :] * begin[d, i, b].astype(F32)
                    + local_v[d, b, g, i * hd : (i + 1) * hd, :]
                ).astype(BF16)
                for d, g, span in blocks
            ]
            for i in (0, 1)
        ]
        growth = [growth_v[d, b, span, :] for d, g, span in blocks]
        scores = [mm(qkv[d, 0, b, span, :], expand(k)) for (d, g, span), k in zip(blocks, keys)]
        scores = [
            w * (score_v[d, b, span, :] + x) for (d, g, span), x, w in zip(blocks, scores, growth)
        ]
        power = [jnp.exp(x - head_max(x)) for x in scores]
        norm = stacked(power)
        weighted = [(x / y * w).astype(BF16) for x, y, w in zip(power, norm, growth)]
        mixing = [
            mm(x, expand(shrink_v[d, b, span, :]), 1, 1) for (d, g, span), x in zip(blocks, weighted)
        ]
        mixing = [(x * causal[d]).astype(BF16) for (d, g, span), x in zip(blocks, mixing)]
        carried = [mm(x, expand(v), 1, 1) for x, v in zip(weighted, values)]
        made = [
            x + mm(y, expand(qkv[d, 2, b, span, :]))
            for (d, g, span), x, y in zip(blocks, carried, mixing)
        ]
        mean = [x / hd for x in stacked([x * x for x in made])]
        made = [x * lax.rsqrt(y + EPSILON) * gain_row for x, y in zip(made, mean)]
        for g in range(spans):
            span = slice(g * SPAN, (g + 1) * SPAN)
            ag[h, b, span, :] = (made[2 * g] + made[2 * g + 1]).astype(BF16)
        attends[b].start()
        if b == 0:
            for member in projection[2:]:
                member.forward()
    attends[0].forward()

    for member in projection:
        member.finish()
    loads[3].wait()
    loads[4].wait()

    masks = [1 << i for i in range(nh.bit_length() - 1)]

    def rs_copy(b, o, m):
        return pltpu.make_async_remote_copy(
            src_ref=pb.at[hx(o), b],
            dst_ref=rb.at[o ^ m, m.bit_length() - 1, b],
            send_sem=rs_s.at[b, o],
            recv_sem=rs_r.at[b, o],
            device_id=(s, hx(m)),
            device_id_type=MESH,
        )

    leaving = sorted(range(nh), key=lambda o: [-((o >> k) & 1) for k in range(len(masks))])

    def level(o):
        return next((k for k, m in enumerate(masks) if o & m), len(masks))

    def settle(b, o):
        total = pf[hx(o), b]
        for k in range(level(o)):
            rs_copy(b, o ^ masks[k], masks[k]).wait_recv()
            total = total + rb[o, k, b].astype(F32)
        if o:
            pb[hx(o), b] = total.astype(BF16)
            rs_copy(b, o, masks[level(o)]).start()
        else:
            out[b] = (res[h, b].astype(F32) + total).astype(BF16)

    wo_all = wo_v[...].reshape(nh * width, nh * width)
    for b in range(batch):
        attends[b].finish()
        attention = jnp.concatenate([ag[j, b] for j in range(nh)], axis=1)
        whole = jnp.concatenate([xg[j, b, HALO : HALO + rows, :] for j in range(nh)], axis=1)
        residual = (whole.astype(F32) + mm(attention, wo_all)).astype(BF16)
        wide = residual.astype(F32)
        for j in range(nh):
            res[j, b] = residual[:, j * width : (j + 1) * width]
        mean = jnp.mean(wide * wide, axis=1, keepdims=True)
        mlp_in = (wide * lax.rsqrt(mean + EPSILON) * gain2[...]).astype(BF16)
        hidden = jax.nn.gelu(mm(mlp_in, up_v[...])).astype(BF16)
        if b + 1 < batch:
            attends[b + 1].forward()
        if b:
            for o in leaving:
                if 0 < level(o) < len(masks):
                    settle(b - 1, o)
        for o in leaving:
            cols = pl.ds(pl.multiple_of(hx(o) * width, width), width)
            made = mm(hidden, dn_v[:, cols])
            if level(o) == 0 and o:
                pb[hx(o), b] = made.astype(BF16)
                rs_copy(b, o, masks[0]).start()
            else:
                pf[hx(o), b] = made
                if o and b == batch - 1:
                    settle(b, o)
    for b in range(batch):
        settle(b, 0)

    tokens.drain()
    for member in projection:
        member.drain()
    for copy in halos:
        copy.wait_send()
    for d in (0, 1):
        for copy in sib_copies(d):
            copy.wait_send()

        @pl.when(jnp.logical_not(last_pair[d]))
        def _():
            for b in range(batch):
                hop_copy(d, b).wait_send()

        for b in range(batch):
            start_copy(d, b).wait_send()

    for b in range(batch):
        attends[b].drain()
        for o in range(1, nh):
            rs_copy(b, o, masks[level(o)]).wait_send()


def local(
    n,
    nh,
    tokens,
    input_norm_gain,
    query_key_value_weight,
    forget_gate_weight,
    convolution_filter_taps,
    slot_forget_rate,
    extra_forget_log,
    head_norm_gain,
    output_projection_weight,
    feedforward_norm_gain,
    up_projection_weight,
    down_projection_weight,
):
    batch, rows, width = tokens.shape
    depth = nh * width
    hidden = up_projection_weight.shape[1]
    spans = rows // SPAN
    hd = head_norm_gain.shape[1]
    tall = rows + 2 * HALO
    vmem = pl.BlockSpec(memory_space=pltpu.VMEM)
    anywhere = pl.BlockSpec(memory_space=pl.ANY)
    dma = pltpu.SemaphoreType.DMA
    bits = nh.bit_length() - 1
    scratch = [
        pltpu.VMEM((nh, batch, tall, width), BF16),
        pltpu.VMEM((3, depth, width), BF16),
        pltpu.VMEM((depth, width), BF16),
        pltpu.VMEM((nh, width, depth), BF16),
        pltpu.VMEM((depth, hidden), BF16),
        pltpu.VMEM((hidden, depth), BF16),
        pltpu.VMEM((batch, tall, depth), BF16),
        pltpu.VMEM((3, batch, tall, width), F32),
        pltpu.VMEM((2, 3, batch, rows, width), BF16),
        pltpu.VMEM((2, batch, rows, width), F32),
        pltpu.VMEM((2, batch, rows, width), BF16),
        pltpu.VMEM((2, batch, rows, width), F32),
        pltpu.VMEM((2, batch, spans, 2 * hd, width), F32),
        pltpu.VMEM((2, batch, spans, width), F32),
        pltpu.VMEM((2, 2, batch, hd, width), BF16),
        pltpu.VMEM((2, batch, hd, width), BF16),
        pltpu.VMEM((2, 8 * pl.cdiv(batch, 8), width), F32),
        pltpu.VMEM((2, 8 * pl.cdiv(batch, 8), width), F32),
        pltpu.VMEM((2, batch, hd, width), F32),
        pltpu.VMEM((2, batch, hd, width), BF16),
        pltpu.VMEM((2, batch, hd, width), BF16),
        pltpu.VMEM((2, batch, hd, width), BF16),
        pltpu.VMEM((2, 2, batch, hd, width), BF16),
        pltpu.VMEM((2, batch, hd, width), F32),
        pltpu.VMEM((2, batch, width), F32),
        pltpu.VMEM((nh, batch, rows, width), BF16),
        pltpu.VMEM((nh, batch, rows, width), BF16),
        pltpu.VMEM((nh, batch, rows, width), F32),
        pltpu.VMEM((nh, batch, rows, width), BF16),
        pltpu.VMEM((nh, bits, batch, rows, width), BF16),
        dma((5,)),
        dma((nh,)),
        dma((nh,)),
        dma((2, nh)),
        dma((2, nh)),
        dma((PIECES, nh)),
        dma((PIECES, nh)),
        dma((2, 2)),
        dma((2, 2)),
        dma((2, batch)),
        dma((2, batch)),
        dma((2, batch)),
        dma((2, batch)),
        dma((batch, nh)),
        dma((batch, nh)),
        dma((batch, nh)),
        dma((batch, nh)),
    ]
    return pl.pallas_call(
        functools.partial(kernel, n, nh),
        out_shape=jax.ShapeDtypeStruct(tokens.shape, tokens.dtype),
        in_specs=[
            vmem,
            vmem,
            anywhere,
            anywhere,
            vmem,
            vmem,
            vmem,
            vmem,
            anywhere,
            vmem,
            anywhere,
            anywhere,
        ],
        out_specs=vmem,
        scratch_shapes=scratch,
        compiler_params=pltpu.CompilerParams(
            collective_id=0, has_side_effects=True, vmem_limit_bytes=56 * 2**20
        ),
        name="layer",
    )(
        tokens,
        input_norm_gain.reshape(1, -1),
        jnp.transpose(query_key_value_weight, (1, 0, 2)),
        forget_gate_weight,
        jnp.transpose(convolution_filter_taps, (0, 2, 1, 3)),
        slot_forget_rate,
        extra_forget_log,
        head_norm_gain,
        output_projection_weight,
        feedforward_norm_gain.reshape(1, -1),
        up_projection_weight,
        down_projection_weight,
    )


def solution(mesh):
    in_specs = (
        P(None, "seq", "head"),
        P(),
        P(None, None, "head"),
        P(None, "head"),
        P(None, None, None, "head"),
        P("head", None),
        P(None, "seq"),
        P("head", None),
        P("head", None),
        P(),
        P(None, "head"),
        P("head", None),
    )
    out_specs = P(None, "seq", "head")
    return jax.shard_map(
        functools.partial(local, mesh.shape["seq"], mesh.shape["head"]),
        mesh=mesh,
        in_specs=in_specs,
        out_specs=out_specs,
        check_vma=False,
    )
```
